128 devices in a mesh: ffn: 32 (over y_hi, x, z), mp: 4 (over y_lo, core).
Axes of the slice: x: 4, y: 4 (y_hi: 2, y_lo: 2; y = y_hi * 2 + y_lo), z: 4, core: 2. Of those that a mesh axis runs over, the one named last changes fastest.
Arguments:
- inputs: bfloat16 [512, 8192], P('ffn', 'mp'), may hold values from -6 to 6
- targets: bfloat16 [512, 8192], P('ffn', 'mp'), may hold values from -3 to 3
- gate_weight: bfloat16 [8192, 16384], P('mp', 'ffn'), may hold values from -0.0625 to 0.0625
- up_weight: bfloat16 [8192, 16384], P('mp', 'ffn'), may hold values from -0.0625 to 0.0625
- down_weight: bfloat16 [16384, 8192], P('ffn', 'mp'), may hold values from -0.046875 to 0.046875
- stored_vectors: bfloat16 [7, 8192, 16384], P(None, 'mp', 'ffn'), may hold values from -12 to 12, as said below
Outputs:
- next_vector: float32 [8192, 16384], P('mp', 'ffn')
- remainder_share: float32 [1], replicated
The draws below stay inside these ranges and needn't reach their ends.
Inputs may be any that keep to these rules, and one draw needn't show every extreme that they name: `stored_vectors`: the last of the 7 vectors is the current Lanczos vector.
All inputs are finite; a program needn't handle non-finite values.
Results may differ from the reference program's by a relative error of at most 0.0049.
Values may be sent and summed in bfloat16 or wider, within the bound.
A program may use at most 128 MiB of HBM per device.

```python
import jax
import jax.numpy as jnp
from jax import lax

D = 8192
FF = 16384
TOKENS = 512
STORED = 7


def draw_stored_vectors(key, part):
    key = jax.random.fold_in(key, 7)
    sizes_drawn = jax.random.uniform(jax.random.fold_in(key, 1000), (STORED - 1,), jnp.float32, 0.15, 0.25)
    signs_drawn = jax.random.rademacher(jax.random.fold_in(key, 1001), (STORED - 1,), jnp.float32)
    mixing = sizes_drawn * signs_drawn
    pieces = []
    last_vector = jnp.zeros((D, FF), jnp.float32)
    for stored_index in range(STORED):
        sub_key = jax.random.fold_in(key, stored_index)
        noise = jnp.clip(jax.random.normal(sub_key, (D, FF), jnp.float32), -6.0, 6.0)
        if stored_index < STORED - 1:
            pieces.append(noise.astype(jnp.bfloat16))
            last_vector = last_vector + mixing[stored_index] * noise
        else:
            last_vector = last_vector + jnp.sqrt(1.0 - jnp.sum(mixing * mixing)) * noise
    pieces.append(last_vector.astype(jnp.bfloat16))
    return jnp.stack(pieces)


def block_levels(rng, extent, shards, smallest, largest):
    def one(position, parts):
        draws = jax.random.uniform(jax.random.fold_in(jax.random.fold_in(rng, 6), position), (parts,), jnp.float32, smallest / len(shards), largest / len(shards))
        return jnp.repeat(jnp.exp(draws), extent[position] // parts).reshape((-1,) + (1,) * (len(extent) - position - 1))

    loudness = one(*shards[0])
    for cut in shards[1:]:
        loudness = loudness * one(*cut)
    return loudness


def gaussian(own_key, extent, spread, most, shards=(), kind=jnp.bfloat16):
    loudness = block_levels(own_key, extent, shards, -0.22, 0.18) if shards else 1.0
    values = jax.random.normal(own_key, extent, jnp.float32) * spread * loudness
    return jnp.minimum(jnp.maximum(values, -most), most).astype(kind)


def setup_inputs(seed: int = 0) -> dict:
    streams_of = jax.random.split(jax.random.key(seed), 7)
    return {
        "inputs": gaussian(streams_of[0], (TOKENS, D), 1.0, 6.0, ((0, 32), (1, 4))),
        "targets": gaussian(streams_of[1], (TOKENS, D), 0.5, 3.0, ((0, 32), (1, 4))),
        "gate_weight": gaussian(streams_of[2], (D, FF), D ** -0.5, 0.0625, ((0, 4), (1, 32))),
        "up_weight": gaussian(streams_of[3], (D, FF), D ** -0.5, 0.0625, ((0, 4), (1, 32))),
        "down_weight": gaussian(streams_of[4], (FF, D), FF ** -0.5, 0.046875, ((0, 32), (1, 4))),
        "stored_vectors": draw_stored_vectors(jax.random.fold_in(streams_of[6], 71), 0),
    }


def solve_small(gram, target_side):
    lower = jnp.linalg.cholesky(gram)
    size_count = target_side.shape[0]
    forward = []
    for row_index in range(size_count):
        running = target_side[row_index]
        for column_index in range(row_index):
            running = running - lower[row_index, column_index] * forward[column_index]
        forward.append(running / lower[row_index, row_index])
    backward = [None] * size_count
    for row_index in reversed(range(size_count)):
        running = forward[row_index]
        for column_index in range(row_index + 1, size_count):
            running = running - lower[column_index, row_index] * backward[column_index]
        backward[row_index] = running / lower[row_index, row_index]
    return jnp.stack(backward)

def reference(inputs, targets, gate_weight, up_weight, down_weight, stored_vectors):
    count = D * FF
    current = stored_vectors[STORED - 1]
    gate = jnp.dot(inputs.astype(jnp.float32), gate_weight.astype(jnp.float32), preferred_element_type=jnp.float32)
    up_values = jnp.dot(inputs.astype(jnp.float32), up_weight.astype(jnp.float32), preferred_element_type=jnp.float32)
    tangent_gate = jnp.dot(inputs.astype(jnp.float32), current.astype(jnp.float32), preferred_element_type=jnp.float32)
    sigmoid_gate = jax.nn.sigmoid(gate)
    swish = gate * sigmoid_gate
    slope = sigmoid_gate * (1.0 + gate * (1.0 - sigmoid_gate))
    curve = sigmoid_gate * (1.0 - sigmoid_gate) * (2.0 + gate * (1.0 - 2.0 * sigmoid_gate))
    hidden = (swish * up_values).astype(jnp.bfloat16)
    tangent_hidden = (slope * up_values * tangent_gate).astype(jnp.bfloat16)
    output = jnp.dot(hidden.astype(jnp.float32), down_weight.astype(jnp.float32), preferred_element_type=jnp.float32)
    tangent_output = jnp.dot(tangent_hidden.astype(jnp.float32), down_weight.astype(jnp.float32), preferred_element_type=jnp.float32)
    residual = (output - targets.astype(jnp.float32)).astype(jnp.bfloat16)
    tangent_residual = tangent_output.astype(jnp.bfloat16)
    grad_hidden = jnp.dot(residual.astype(jnp.float32), down_weight.T.astype(jnp.float32), preferred_element_type=jnp.float32)
    tangent_grad = jnp.dot(tangent_residual.astype(jnp.float32), down_weight.T.astype(jnp.float32), preferred_element_type=jnp.float32)
    adjoint = (tangent_grad * up_values * slope + grad_hidden * up_values * curve * tangent_gate).astype(jnp.bfloat16)
    image = lax.dot_general(inputs.astype(jnp.float32), adjoint.astype(jnp.float32), (((0,), (0,)), ((), ())), preferred_element_type=jnp.float32)
    correlations = lax.map(lambda stored: jnp.sum(stored.astype(jnp.float32) * image), stored_vectors) / count
    flattened = stored_vectors.reshape(STORED, count)
    gram = lax.dot_general(flattened.astype(jnp.float32), flattened.astype(jnp.float32), (((1,), (1,)), ((), ())), preferred_element_type=jnp.float32) / count
    power = jnp.sum(image * image) / count
    loadings = solve_small(gram, correlations)
    remainder = image
    for stored_index in range(STORED):
        remainder = remainder - loadings[stored_index] * stored_vectors[stored_index].astype(jnp.float32)
    rest = jnp.sum(remainder * remainder) / count
    next_vector = remainder / jnp.sqrt(rest + 1e-06)
    remainder_share = jnp.sqrt((rest + 1e-06) / (power + 1e-06)).reshape(1)
    return (next_vector, remainder_share)
```

```python
import functools

import jax
import jax.numpy as jnp
from jax import lax
from jax.experimental import pallas as pl
from jax.experimental.pallas import tpu as pltpu
from jax.sharding import PartitionSpec as P

D = 8192
FF = 16384
STORED = 7
MESH = pl.DeviceIdType.MESH
F32 = jnp.float32
BF16 = jnp.bfloat16
PAIRS = [(j, k) for j in range(STORED) for k in range(j, STORED)]
N_GRAM = len(PAIRS)
STAT_ROWS = 40

B_Y = F32
C1 = BF16
C2 = BF16
C3 = F32


def dot(left, right):
    return jnp.dot(left, right, preferred_element_type=F32)


def dot_nt(left, right):
    return lax.dot_general(left, right, (((1,), (1,)), ((), ())), preferred_element_type=F32)


def fold(values):
    rows = values.shape[0]
    part = jnp.sum(values.reshape(rows // 8, 8, 512), axis=0)
    part = part[:, 0:128] + part[:, 128:256] + part[:, 256:384] + part[:, 384:512]
    return jnp.sum(part, axis=0, keepdims=True)


def comm_kernel(
    x_hbm, tgt_hbm, gate_hbm, up_hbm, down_hbm, stored_hbm,
    adj_out, x_out, coef_out,
    xg, tgt, gate_w, up_w, down_w, st,
    part, rb, sby, rby, tmat, gx,
    hp, a_q, b_q,
    s1, r1, s2, r2, s3, r3, rp,
    gacc, rg, sy, ry, adj,
    stat, stat_r, stat_x, stat_z,
    lsem, ssem, rsem,
):
    f = lax.axis_index("ffn")
    m = lax.axis_index("mp")
    yh, x, z = f // 16, (f // 4) % 4, f % 4
    yl, c = m // 2, m % 2
    q = c * 2 + yl
    qy = c * 2 + (1 - yl)

    def at(yh_=yh, x_=x, z_=z, yl_=yl, c_=c):
        return (yh_ * 16 + x_ * 4 + z_, yl_ * 2 + c_)

    p_core, p_yl, p_yh = at(c_=1 - c), at(yl_=1 - yl), at(yh_=1 - yh)
    xs = [(x + d) % 4 for d in (1, 2, 3)]
    zs = [(z + d) % 4 for d in (1, 2, 3)]
    p_x = [at(x_=v) for v in xs]
    p_z = [at(z_=v) for v in zs]
    peers = [p_core, p_yl, p_yh] + p_x + p_z

    counter = [0]

    def remote(src, dst, who):
        i = counter[0]
        counter[0] += 1
        return pltpu.make_async_remote_copy(
            src_ref=src, dst_ref=dst, send_sem=ssem.at[i], recv_sem=rsem.at[i],
            device_id=who, device_id_type=MESH,
        )

    def go(*copies):
        for copy in copies:
            copy.start()
        return list(copies)

    sent = []

    def go_sent(*copies):
        sent.extend(go(*copies))
        return list(copies)

    loads = [
        pltpu.make_async_copy(x_hbm.at[:, pl.ds(h * 1024, 1024)], xg.at[h, yh, x, z], lsem.at[h])
        for h in range(2)
    ]
    late = [
        pltpu.make_async_copy(stored_hbm, st, lsem.at[2]),
        pltpu.make_async_copy(gate_hbm, gate_w, lsem.at[3]),
        pltpu.make_async_copy(up_hbm, up_w, lsem.at[4]),
        pltpu.make_async_copy(down_hbm, down_w, lsem.at[5]),
        pltpu.make_async_copy(tgt_hbm, tgt, lsem.at[6]),
    ]
    go(*loads)
    go(*late)

    barrier = pltpu.get_barrier_semaphore()
    for who in peers:
        pl.semaphore_signal(barrier, inc=1, device_id=who, device_id_type=MESH)
    pl.semaphore_wait(barrier, len(peers))
    for copy in loads:
        copy.wait()

    def block(ref, h, yh_):
        return ref.at[h, yh_, x, z]

    a1 = go_sent(remote(xg.at[:, yh, x, z], xg.at[:, yh, x, z], p_yh))
    a2 = []
    for d in range(3):
        a2 += go_sent(
            remote(block(xg, 0, yh), block(xg, 0, yh), p_z[d]),
            remote(block(xg, 1, yh), block(xg, 1, yh), p_x[d]),
        )
    a1[0].wait_recv()
    for d in range(3):
        a2 += go_sent(
            remote(block(xg, 0, 1 - yh), block(xg, 0, 1 - yh), p_z[d]),
            remote(block(xg, 1, 1 - yh), block(xg, 1, 1 - yh), p_x[d]),
        )

    late[0].wait()

    def gram_range(first, last, accs):
        def step(i, accs):
            row = pl.multiple_of(i * 16, 16)
            accs = list(accs)
            for col in range(4):
                v = [
                    st[k, pl.ds(row, 16), col * 128:(col + 1) * 128].astype(F32)
                    for k in range(STORED)
                ]
                for n, (j, k) in enumerate(PAIRS):
                    prod = v[j] * v[k]
                    accs[n] = accs[n] + prod[0:8] + prod[8:16]
            return tuple(accs)

        return lax.fori_loop(first, last, step, accs)

    accs = tuple(jnp.zeros((8, 128), F32) for _ in PAIRS)
    accs = gram_range(0, 32, accs)
    for copy in a2:
        copy.wait_recv()
    a3 = []
    for d in range(3):
        a3 += go_sent(
            remote(xg.at[0, :, x], xg.at[0, :, x], p_x[d]),
            remote(xg.at[1, :, :, z], xg.at[1, :, :, z], p_z[d]),
        )
    accs = gram_range(32, 128, accs)
    for n in range(N_GRAM):
        stat[n:n + 1, :] = jnp.sum(accs[n], axis=0, keepdims=True)
    for copy in late[1:]:
        copy.wait()
    for copy in a3:
        copy.wait_recv()

    def x_rows(h, half):
        return xg[h, half].reshape(256, 1024)

    def partial(half):
        def step(n, carry):
            col = pl.multiple_of(n * 256, 256)
            cols = pl.ds(col, 256)
            left0, left1 = x_rows(0, half), x_rows(1, half)
            part[0, half, :, cols] = dot(left0, gate_w[0:1024, cols]) + dot(left1, gate_w[1024:2048, cols])
            part[1, half, :, cols] = dot(left0, up_w[0:1024, cols]) + dot(left1, up_w[1024:2048, cols])
            part[2, half, :, cols] = dot(left0, st[6, 0:1024, cols]) + dot(left1, st[6, 1024:2048, cols])
            return carry

        lax.fori_loop(0, 2, step, 0)

    partial(1 - c)
    b1 = go_sent(remote(part.at[:, 1 - c], rb, p_core))
    partial(c)
    b1[0].wait_recv()
    own = pl.ds(pl.multiple_of(yl * 128, 128), 128)
    other = pl.ds(pl.multiple_of((1 - yl) * 128, 128), 128)
    for n in range(3):
        sby[n] = (part[n, c, other, :] + rb[n, other, :]).astype(B_Y)
    b2 = go_sent(remote(sby, rby, p_yl))
    for n in range(3):
        rb[n, own, :] = rb[n, own, :] + part[n, c, own, :]
    b2[0].wait_recv()
    gate = rb[0, own, :] + rby[0].astype(F32)
    upv = rb[1, own, :] + rby[1].astype(F32)
    tang = rb[2, own, :] + rby[2].astype(F32)
    sg = 1.0 / (1.0 + jnp.exp(-gate))
    swish = gate * sg
    slope = sg * (1.0 + gate * (1.0 - sg))
    curve = sg * (1.0 - sg) * (2.0 + gate * (1.0 - 2.0 * sg))
    hp[0, q] = (swish * upv).astype(BF16)
    hp[1, q] = (slope * upv * tang).astype(BF16)
    a_q[...] = upv * slope
    b_q[...] = upv * curve * tang
    b3 = go_sent(
        remote(hp.at[:, q], hp.at[:, q], p_yl),
        remote(hp.at[:, q], hp.at[:, q], p_core),
    )
    b3[0].wait_recv()
    b4 = go_sent(remote(hp.at[:, qy], hp.at[:, qy], p_core))
    b3[1].wait_recv()
    b4[0].wait_recv()

    c1 = []
    for h in range(2):
        def out_step(i, carry, h=h):
            r = i // 4
            col = pl.multiple_of((i % 4) * 256, 256)
            left = hp[r // 2, pl.ds((r % 2) * 2, 2)].reshape(256, 512)
            right = down_w[:, pl.ds(pl.multiple_of(h * 1024 + col, 256), 256)]
            s1[h, r, :, :, :, pl.ds(col, 256)] = dot(left, right).astype(C1).reshape(4, 4, 16, 256)
            return carry

        lax.fori_loop(0, 16, out_step, 0)
        for d in range(3):
            if h == 0:
                c1 += go_sent(remote(s1.at[0, :, :, zs[d]], r1.at[0, d], p_z[d]))
            else:
                c1 += go_sent(remote(s1.at[1, :, xs[d]], r1.at[1, d], p_x[d]))

    def tm_step(i, carry):
        k = i // 4
        half = (i // 2) % 2
        cols = pl.ds(pl.multiple_of((i % 2) * 256, 256), 256)
        tmat[k, pl.ds(pl.multiple_of(half * 256, 256), 256), cols] = (
            dot(x_rows(0, half), st[k, 0:1024, cols]) + dot(x_rows(1, half), st[k, 1024:2048, cols])
        )
        return carry

    lax.fori_loop(0, 24, tm_step, 0)

    def gx_step(i, carry):
        r, s = i // 2, i % 2
        value = dot_nt(x_rows(0, r), x_rows(0, s)) + dot_nt(x_rows(1, r), x_rows(1, s))
        rows = pl.ds(pl.multiple_of(r * 256, 256), 256)
        cols = pl.ds(pl.multiple_of(s * 256, 256), 256)
        high = value.astype(BF16)
        gx[0, rows, cols] = high
        gx[1, rows, cols] = (value - high.astype(F32)).astype(BF16)
        return carry

    lax.fori_loop(0, 4, gx_step, 0)

    xo = pltpu.make_async_copy(xg, x_out, lsem.at[7])
    xo.start()

    c2 = []
    for h in range(2):
        for d in range(3):
            c1[h * 3 + d].wait_recv()

        def sum_step(i, carry, h=h):
            r, g = i // 4, i % 4
            mine = s1[0, r, g, z] if h == 0 else s1[1, r, x, g]
            total = mine.astype(F32)
            for d in range(3):
                total = total + r1[h, d, r, g].astype(F32)
            s2[h, r, g] = total.astype(C2)
            return carry

        lax.fori_loop(0, 16, sum_step, 0)
        for d in range(3):
            if h == 0:
                c2 += go_sent(remote(s2.at[0, :, xs[d]], r2.at[0, d], p_x[d]))
            else:
                c2 += go_sent(remote(s2.at[1, :, zs[d]], r2.at[1, d], p_z[d]))
    for copy in c2:
        copy.wait_recv()
    for h in range(2):
        for p in range(2):
            for w in range(2):
                r = p * 2 + w
                mine = s2[0, r, x] if h == 0 else s2[1, r, z]
                total = mine.astype(F32)
                for d in range(3):
                    total = total + r2[h, d, r].astype(F32)
                s3[h, p, w] = total.astype(C3)
    c3 = go_sent(remote(s3.at[:, :, 1 - yh], r3, p_yh))
    c3[0].wait_recv()
    for h in range(2):
        for p in range(2):
            total = s3[h, p, yh].astype(F32) + r3[h, p].astype(F32)
            if p == 0:
                total = total - tgt[:, h * 1024:(h + 1) * 1024].astype(F32)
            rp[h, p, yh, x, z] = total.astype(BF16)

    own_rp = rp.at[:, :, yh, x, z]
    d1 = go_sent(remote(own_rp, own_rp, p_yh))
    d1[0].wait_recv()
    d2 = []
    for d in range(3):
        for h in range(2):
            ref = rp.at[h, :, :, x, z]
            d2 += go_sent(remote(ref, ref, (p_x, p_z)[h][d]))
    for copy in d2:
        copy.wait_recv()
    d3 = []
    for d in range(3):
        ref0, ref1 = rp.at[0, :, :, :, z], rp.at[1, :, :, x]
        d3 += go_sent(remote(ref0, ref0, p_z[d]), remote(ref1, ref1, p_x[d]))
    for copy in d3:
        copy.wait_recv()

    def grad(half):
        for p in range(2):
            def step(n, carry, p=p):
                cols = pl.ds(pl.multiple_of(n * 256, 256), 256)
                value = dot_nt(rp[0, p, half].reshape(256, 1024), down_w[cols, 0:1024])
                value = value + dot_nt(rp[1, p, half].reshape(256, 1024), down_w[cols, 1024:2048])
                gacc[p, half, :, cols] = value
                return carry

            lax.fori_loop(0, 2, step, 0)

    grad(1 - c)
    e1 = go_sent(remote(gacc.at[:, 1 - c], rg, p_core))
    grad(c)
    e1[0].wait_recv()
    for p in range(2):
        sy[p] = gacc[p, c, other, :] + rg[p, other, :]
    e2 = go_sent(remote(sy, ry, p_yl))
    e2[0].wait_recv()
    gh = gacc[0, c, own, :] + rg[0, own, :] + ry[0]
    tg = gacc[1, c, own, :] + rg[1, own, :] + ry[1]
    adj[q] = (tg * a_q[...] + gh * b_q[...]).astype(BF16)
    e3 = go_sent(
        remote(adj.at[q], adj.at[q], p_yl),
        remote(adj.at[q], adj.at[q], p_core),
    )
    e3[0].wait_recv()
    e4 = go_sent(remote(adj.at[qy], adj.at[qy], p_core))
    e3[1].wait_recv()
    e4[0].wait_recv()
    ao = pltpu.make_async_copy(adj, adj_out, lsem.at[8])
    ao.start()

    for k in range(STORED):
        total = jnp.zeros((1, 128), F32)
        for i in range(4):
            left = part[2, i // 2, (i % 2) * 128:(i % 2) * 128 + 128, :] if k == 6 else tmat[k, i * 128:i * 128 + 128, :]
            total = total + fold(left * adj[i].astype(F32))
        stat[N_GRAM + k:N_GRAM + k + 1, :] = total
    whole = adj[...].reshape(512, 512)
    total = jnp.zeros((1, 128), F32)
    for i in range(2):
        rows = slice(i * 256, i * 256 + 256)
        mixed = dot(gx[0, rows, :], whole) + dot(gx[1, rows, :], whole)
        total = total + fold(mixed * whole[i * 256:i * 256 + 256].astype(F32))
    stat[N_GRAM + 7:N_GRAM + 8, :] = total
    stat[N_GRAM + 8:STAT_ROWS, :] = jnp.zeros((STAT_ROWS - N_GRAM - 8, 128), F32)

    for n, who in enumerate((p_core, p_yl, p_yh)):
        sc = go_sent(remote(stat.at[pl.ds(n * STAT_ROWS, STAT_ROWS)], stat_r.at[n], who))
        sc[0].wait_recv()
        both = stat[n * STAT_ROWS:(n + 1) * STAT_ROWS, :] + stat_r[n]
        if n < 2:
            stat[(n + 1) * STAT_ROWS:(n + 2) * STAT_ROWS, :] = both
    stat_x[x] = both
    sc = go_sent(*[remote(stat_x.at[x], stat_x.at[x], p_x[d]) for d in range(3)])
    for copy in sc:
        copy.wait_recv()
    stat_z[z] = (stat_x[0] + stat_x[1]) + (stat_x[2] + stat_x[3])
    sc = go_sent(*[remote(stat_z.at[z], stat_z.at[z], p_z[d]) for d in range(3)])
    for copy in sc:
        copy.wait_recv()
    total = (stat_z[0] + stat_z[1]) + (stat_z[2] + stat_z[3])
    means = jnp.sum(total, axis=1, keepdims=True) * (1.0 / (D * FF))
    value = [means[n:n + 1, :] for n in range(N_GRAM + 8)]
    gram = {}
    for n, (j, k) in enumerate(PAIRS):
        gram[j, k] = gram[k, j] = value[n]
    corr = value[N_GRAM:N_GRAM + 7]
    power = value[N_GRAM + 7]
    lower = {}
    inverse = []
    for j in range(STORED):
        pivot = gram[j, j]
        for n in range(j):
            pivot = pivot - lower[j, n] * lower[j, n]
        pivot = jnp.sqrt(pivot)
        inverse.append(1.0 / pivot)
        for i in range(j + 1, STORED):
            entry = gram[i, j]
            for n in range(j):
                entry = entry - lower[i, n] * lower[j, n]
            lower[i, j] = entry * inverse[j]
    forward = []
    for j in range(STORED):
        running = corr[j]
        for n in range(j):
            running = running - lower[j, n] * forward[n]
        forward.append(running * inverse[j])
    load = [None] * STORED
    for j in reversed(range(STORED)):
        running = forward[j]
        for n in range(j + 1, STORED):
            running = running - lower[n, j] * load[n]
        load[j] = running * inverse[j]
    rest = power
    for j in range(STORED):
        inner = -2.0 * corr[j]
        for k in range(STORED):
            inner = inner + gram[j, k] * load[k]
        rest = rest + load[j] * inner
    rest = jnp.maximum(rest, 0.0)
    scale = 1.0 / jnp.sqrt(rest + 1e-06)
    share = jnp.sqrt((rest + 1e-06) / (power + 1e-06))
    rows = [-(load[j] * scale) for j in range(STORED)] + [scale, share]
    rows = rows + [jnp.zeros((1, 1), F32)] * (16 - len(rows))
    for n in range(16):
        coef_out[n:n + 1, :] = jnp.broadcast_to(rows[n], (1, 128))

    for copy in sent:
        copy.wait_send()
    xo.wait()
    ao.wait()


def final_kernel(coef, x_ref, adj_ref, st_ref, out_ref, share_ref):
    @pl.when(pl.program_id(0) == 0)
    def _():
        share_ref[0] = coef[8, 0]

    left = x_ref[0].reshape(512, x_ref.shape[-1])
    image = lax.dot_general(
        left, adj_ref[...], (((0,), (0,)), ((), ())), preferred_element_type=F32
    )
    total = image * coef[7, 0]
    for k in range(STORED):
        total = total + coef[k, 0] * st_ref[k].astype(F32)
    out_ref[...] = total


def body(inputs, targets, gate_weight, up_weight, down_weight, stored_vectors):
    any_spec = pl.BlockSpec(memory_space=pl.ANY)
    n_copies = 70
    adj, xg, coef = pl.pallas_call(
        comm_kernel,
        out_shape=(
            jax.ShapeDtypeStruct((4, 128, 512), BF16),
            jax.ShapeDtypeStruct((2, 2, 4, 4, 16, 1024), BF16),
            jax.ShapeDtypeStruct((16, 128), F32),
        ),
        in_specs=[any_spec] * 6,
        out_specs=(any_spec, any_spec, pl.BlockSpec(memory_space=pltpu.VMEM)),
        scratch_shapes=[
            pltpu.VMEM((2, 2, 4, 4, 16, 1024), BF16),
            pltpu.VMEM((16, 2048), BF16),
            pltpu.VMEM((2048, 512), BF16),
            pltpu.VMEM((2048, 512), BF16),
            pltpu.VMEM((512, 2048), BF16),
            pltpu.VMEM((STORED, 2048, 512), BF16),
            pltpu.VMEM((3, 2, 256, 512), F32),
            pltpu.VMEM((3, 256, 512), F32),
            pltpu.VMEM((3, 128, 512), B_Y),
            pltpu.VMEM((3, 128, 512), B_Y),
            pltpu.VMEM((STORED - 1, 512, 512), F32),
            pltpu.VMEM((2, 512, 512), BF16),
            pltpu.VMEM((2, 4, 128, 512), BF16),
            pltpu.VMEM((128, 512), F32),
            pltpu.VMEM((128, 512), F32),
            pltpu.VMEM((2, 4, 4, 4, 16, 1024), C1),
            pltpu.VMEM((2, 3, 4, 4, 16, 1024), C1),
            pltpu.VMEM((2, 4, 4, 16, 1024), C2),
            pltpu.VMEM((2, 3, 4, 16, 1024), C2),
            pltpu.VMEM((2, 2, 2, 16, 1024), C3),
            pltpu.VMEM((2, 2, 16, 1024), C3),
            pltpu.VMEM((2, 2, 2, 4, 4, 16, 1024), BF16),
            pltpu.VMEM((2, 2, 256, 512), F32),
            pltpu.VMEM((2, 256, 512), F32),
            pltpu.VMEM((2, 128, 512), F32),
            pltpu.VMEM((2, 128, 512), F32),
            pltpu.VMEM((4, 128, 512), BF16),
            pltpu.VMEM((3 * STAT_ROWS, 128), F32),
            pltpu.VMEM((3, STAT_ROWS, 128), F32),
            pltpu.VMEM((4, STAT_ROWS, 128), F32),
            pltpu.VMEM((4, STAT_ROWS, 128), F32),
            pltpu.SemaphoreType.DMA((9,)),
            pltpu.SemaphoreType.DMA((n_copies,)),
            pltpu.SemaphoreType.DMA((n_copies,)),
        ],
        compiler_params=pltpu.CompilerParams(
            collective_id=0, has_side_effects=True, vmem_limit_bytes=62 * 2**20
        ),
        name="exchange",
    )(inputs, targets, gate_weight, up_weight, down_weight, stored_vectors)

    tile = 128
    per_half = 1024 // tile
    next_vector, share = pl.pallas_call(
        final_kernel,
        grid=(2048 // tile,),
        out_shape=(
            jax.ShapeDtypeStruct((2048, 512), F32),
            jax.ShapeDtypeStruct((1,), F32),
        ),
        in_specs=[
            pl.BlockSpec(memory_space=pltpu.SMEM),
            pl.BlockSpec((1, 512, tile), lambda i: (i // per_half, 0, i % per_half)),
            pl.BlockSpec((512, 512), lambda i: (0, 0)),
            pl.BlockSpec((STORED, tile, 512), lambda i: (0, i, 0)),
        ],
        out_specs=(
            pl.BlockSpec((tile, 512), lambda i: (i, 0)),
            pl.BlockSpec(memory_space=pltpu.SMEM),
        ),
        compiler_params=pltpu.CompilerParams(vmem_limit_bytes=32 * 2**20),
        name="finish",
    )(coef, xg.reshape(2, 512, 1024), adj.reshape(512, 512), stored_vectors)
    return next_vector, share


def solution(mesh):
    return jax.shard_map(
        body,
        mesh=mesh,
        in_specs=(
            P("ffn", "mp"),
            P("ffn", "mp"),
            P("mp", "ffn"),
            P("mp", "ffn"),
            P("ffn", "mp"),
            P(None, "mp", "ffn"),
        ),
        out_specs=(P("mp", "ffn"), P()),
        check_vma=False,
    )
```

```python
import functools

import jax
import jax.numpy as jnp
from jax import lax
from jax.experimental import pallas as pl
from jax.experimental.pallas import tpu as pltpu
from jax.sharding import PartitionSpec as P

D = 8192
FF = 16384
STORED = 7
MESH = pl.DeviceIdType.MESH
F32 = jnp.float32
BF16 = jnp.bfloat16
PAIRS = [(j, k) for j in range(STORED) for k in range(j, STORED)]
N_GRAM = len(PAIRS)

B_Y = BF16
C1 = BF16
C2 = BF16
C3 = BF16
E_Y = BF16
S = 4
W = 1024 // S
J = 2


def dot(left, right):
    return jnp.dot(left, right, preferred_element_type=F32)


def dot_nt(left, right):
    return lax.dot_general(left, right, (((1,), (1,)), ((), ())), preferred_element_type=F32)


def fold(values):
    rows, lanes = values.shape
    part = jnp.sum(values.reshape(rows // 8, 8, lanes), axis=0)
    total = part[:, 0:128]
    for n in range(1, lanes // 128):
        total = total + part[:, n * 128:n * 128 + 128]
    return jnp.sum(total, axis=0, keepdims=True)


def comm_kernel(
    x_hbm, tgt_hbm, gate_hbm, up_hbm, down_hbm, stored_hbm,
    adj_out, x_out, coef_out,
    xg, tgt, gate_w, up_w, down_w, st,
    part, rb, sby, rby, tmat, gx,
    hp, ab, s1, r1, s2, s2_own, r2, s3, s3_own, r3, rp,
    gacc, pa, rg, sy, ry, adj,
    stat_g, slot_gy, slot_gx, stat_c, slot_cy, slot_cx,
    lsem, ssem, rsem,
):
    f = lax.axis_index("ffn")
    m = lax.axis_index("mp")
    yh, x, z = f // 16, (f // 4) % 4, f % 4
    yl, c = m // 2, m % 2
    q = c * 2 + yl
    qy = c * 2 + (1 - yl)

    def at(yh_=yh, x_=x, z_=z, yl_=yl, c_=c):
        return (yh_ * 16 + x_ * 4 + z_, yl_ * 2 + c_)

    xs = [(x + d) % 4 for d in (1, 3, 2)]
    zs = [(z + d) % 4 for d in (1, 3, 2)]
    p_x = [at(x_=v) for v in xs]
    p_z = [at(z_=v) for v in zs]
    p_yc = [
        at(yh_=(yh + i) % 2, yl_=(yl + j) % 2, c_=(c + k) % 2)
        for i in range(2) for j in range(2) for k in range(2) if i + j + k > 0
    ]
    p_xz = [
        at(x_=(x + i) % 4, z_=(z + j) % 4) for i in range(4) for j in range(4) if i + j > 0
    ]
    p_core, p_yl, p_yh = at(c_=1 - c), at(yl_=1 - yl), at(yh_=1 - yh)
    peers = p_yc + p_xz

    counter = [0]

    def remote(src, dst, who):
        i = counter[0]
        counter[0] += 1
        return pltpu.make_async_remote_copy(
            src_ref=src, dst_ref=dst, send_sem=ssem.at[i], recv_sem=rsem.at[i],
            device_id=who, device_id_type=MESH,
        )

    sent = []

    def go(*copies):
        for copy in copies:
            copy.start()
        return list(copies)

    def go_sent(*copies):
        sent.extend(go(*copies))
        return list(copies)

    loads = [
        pltpu.make_async_copy(x_hbm.at[:, pl.ds(h * 1024, 1024)], xg.at[h, yh, x, z], lsem.at[h])
        for h in range(2)
    ]
    late = [
        pltpu.make_async_copy(gate_hbm, gate_w, lsem.at[2]),
        pltpu.make_async_copy(up_hbm, up_w, lsem.at[3]),
        pltpu.make_async_copy(stored_hbm, st, lsem.at[4]),
        pltpu.make_async_copy(down_hbm, down_w, lsem.at[5]),
        pltpu.make_async_copy(tgt_hbm, tgt, lsem.at[6]),
    ]
    go(*loads)
    go(*late)

    barrier = pltpu.get_barrier_semaphore()
    for who in peers:
        pl.semaphore_signal(barrier, inc=1, device_id=who, device_id_type=MESH)
    for j in range(J):
        for n in range(3):
            part[j, n] = jnp.zeros(part.shape[2:], F32)
    pl.semaphore_wait(barrier, len(peers))
    for copy in loads:
        copy.wait()

    def block(h, yh_):
        return xg.at[h, yh_, x, z]

    a1 = go_sent(remote(xg.at[:, yh, x, z], xg.at[:, yh, x, z], p_yh))
    a2 = {}
    a3 = {}

    def second(i, w):
        a2[i] = []
        for d in range(3):
            a2[i] += go_sent(
                remote(block(0, w), block(0, w), p_z[d]),
                remote(block(1, w), block(1, w), p_x[d]),
            )

    def third(i, w):
        for copy in a2[i]:
            copy.wait_recv()
        a3[i] = []
        for d in range(3):
            a3[i] += go_sent(
                remote(xg.at[0, w, x], xg.at[0, w, x], p_x[d]),
                remote(xg.at[1, w, :, z], xg.at[1, w, :, z], p_z[d]),
            )

    mine, far = yh, 1 - yh
    second(0, mine)
    a1[0].wait_recv()
    second(1, far)
    third(0, mine)
    third(1, far)
    for copy in late:
        copy.wait()

    def partial(h, line):
        def step(j, carry):
            cols = pl.ds(pl.multiple_of(j * 256, 256), 256)
            left = (xg[0, :, line] if h == 0 else xg[1, :, :, line]).reshape(128, 1024)
            depth = slice(h * 1024, h * 1024 + 1024)
            for n in range(3):
                right = (gate_w, up_w)[n][depth, cols] if n < 2 else st[6, depth, cols]
                value = dot(left, right).reshape(2, 4, 16, 256)
                if h == 0:
                    part[j, n, :, line] = part[j, n, :, line] + value
                else:
                    part[j, n, :, :, line] = part[j, n, :, :, line] + value
            return carry

        lax.fori_loop(0, J, step, 0)

    partial(0, x)
    partial(1, z)
    for d, source in ((0, 1), (1, 0), (2, 2)):
        a3[0][2 * d].wait_recv()
        a3[1][2 * d].wait_recv()
        partial(0, xs[source])
        a3[0][2 * d + 1].wait_recv()
        a3[1][2 * d + 1].wait_recv()
        partial(1, zs[source])

    b1 = []
    for j in range(J):
        b1 += go_sent(remote(part.at[j, :, 1 - c], rb.at[j], p_core))
    b2 = []
    for j in range(J):
        b1[j].wait_recv()
        for n in range(3):
            for i in range(2):
                g = (1 - yl) * 2 + i
                sby[j, n, i] = (part[j, n, c, g] + rb[j, n, g]).astype(B_Y)
        b2 += go_sent(remote(sby.at[j], rby.at[j], p_yl))
    b3 = []
    for j in range(J):
        cols = slice(j * 256, j * 256 + 256)
        sums = []
        b2[j].wait_recv()
        for n in range(3):
            halves = []
            for i in range(2):
                g = yl * 2 + i
                halves.append(part[j, n, c, g] + rb[j, n, g] + rby[j, n, i].astype(F32))
            sums.append(jnp.concatenate([v.reshape(64, 256) for v in halves], axis=0))
        gate, upv, tang = sums
        sg = 1.0 / (1.0 + jnp.exp(-gate))
        swish = gate * sg
        slope = sg * (1.0 + gate * (1.0 - sg))
        curve = sg * (1.0 - sg) * (2.0 + gate * (1.0 - 2.0 * sg))
        hp[j, 0, q] = (swish * upv).astype(BF16)
        hp[j, 1, q] = (slope * upv * tang).astype(BF16)
        ref = hp.at[j, :, q]
        b3.append(go_sent(remote(ref, ref, p_yl), remote(ref, ref, p_core)))
        ab[0, q, :, cols] = upv * slope
        ab[1, q, :, cols] = upv * curve * tang
    b4 = []
    for j in range(J):
        b3[j][0].wait_recv()
        ref = hp.at[j, :, qy]
        b4 += go_sent(remote(ref, ref, p_core))
    for j in range(J):
        b3[j][1].wait_recv()
        b4[j].wait_recv()

    own_ab = ab.at[:, q]
    ab1 = go_sent(remote(own_ab, own_ab, p_yl), remote(own_ab, own_ab, p_core))
    c1, c2, c3, d1, d2, d3, d4 = {}, {}, {}, {}, {}, {}, {}

    def c1_issue(s):
        c1[s] = []
        for h in range(2):
            def out_step(r, carry, h=h):
                wide = slice(h * 1024 + s * W, h * 1024 + s * W + W)
                value = jnp.zeros((256, W), F32)
                for j in range(J):
                    left = hp[j, r // 2, pl.ds((r % 2) * 2, 2)].reshape(256, 256)
                    value = value + dot(left, down_w[j * 256:j * 256 + 256, wide])
                s1[s, h, r] = value.astype(C1).reshape(4, 4, 16, W)
                return carry

            lax.fori_loop(0, 4, out_step, 0)
            for d in range(3):
                if h == 0:
                    c1[s] += go_sent(remote(s1.at[s, 0, :, :, zs[d]], r1.at[s, 0, d], p_z[d]))
                else:
                    c1[s] += go_sent(remote(s1.at[s, 1, :, xs[d]], r1.at[s, 1, d], p_x[d]))

    def c2_issue(s):
        for h in range(2):
            for d in range(3):
                c1[s][h * 3 + d].wait_recv()

            def sum_step(i, carry, h=h):
                p, g = i // 4, i % 4
                for own in range(2):
                    w = yh if own else 1 - yh
                    r = p * 2 + w
                    here = s1[s, 0, r, g, z] if h == 0 else s1[s, 1, r, x, g]
                    total = here.astype(F32)
                    for d in range(3):
                        total = total + r1[s, h, d, r, g].astype(F32)
                    if own:
                        s2_own[s, h, p, g] = total
                    else:
                        s2[s, h, p, g] = total.astype(C2)
                return carry

            lax.fori_loop(0, 8, sum_step, 0)
        c2[s] = go_sent(remote(s2.at[s], r2.at[s], p_yh))

    def c3_issue(s):
        c2[s][0].wait_recv()
        c3[s] = []
        for h in range(2):
            for p in range(2):
                total = s2_own[s, h, p] + r2[s, h, p].astype(F32)
                s3_own[s, h, p] = total
                s3[s, h, p] = total.astype(C3)
            for d in range(3):
                if h == 0:
                    c3[s] += go_sent(remote(s3.at[s, 0, :, xs[d]], r3.at[s, 0, d], p_x[d]))
                else:
                    c3[s] += go_sent(remote(s3.at[s, 1, :, zs[d]], r3.at[s, 1, d], p_z[d]))

    def d1_issue(s):
        for copy in c3[s]:
            copy.wait_recv()
        d1[s] = []
        for h in range(2):
            for p in range(2):
                total = s3_own[s, h, p, x if h == 0 else z]
                for d in range(3):
                    total = total + r3[s, h, d, p].astype(F32)
                if p == 0:
                    wide = slice(h * 1024 + s * W, h * 1024 + s * W + W)
                    total = total - tgt[:, wide].astype(F32)
                rp[s, h, p, yh, x, z] = total.astype(BF16)
            ref = rp.at[s, h, :, yh, x, z]
            for d in range(3):
                d1[s] += go_sent(remote(ref, ref, (p_x, p_z)[h][d]))

    def d2_issue(s):
        for copy in d1[s]:
            copy.wait_recv()
        ref0, ref1 = rp.at[s, 0, :, yh, :, z], rp.at[s, 1, :, yh, x]
        d2[s] = go_sent(remote(ref0, ref0, p_yh), remote(ref1, ref1, p_yh))

    def d3_issue(s):
        for copy in d2[s]:
            copy.wait_recv()
        d3[s] = []
        for d in range(2):
            ref0, ref1 = rp.at[s, 0, :, :, :, z], rp.at[s, 1, :, :, x]
            d3[s] += go_sent(remote(ref0, ref0, p_z[d]), remote(ref1, ref1, p_x[d]))

    def d4_issue(s):
        d4[s] = []
        for d in range(2):
            d3[s][2 * d].wait_recv()
            ref = rp.at[s, 0, d, :, :, zs[1 - d]]
            d4[s] += go_sent(remote(ref, ref, p_z[d]))
            d3[s][2 * d + 1].wait_recv()
            ref = rp.at[s, 1, d, :, xs[1 - d]]
            d4[s] += go_sent(remote(ref, ref, p_x[d]))

    c1_issue(0)
    c1_issue(1)

    def x_rows(h, half):
        return xg[h, half].reshape(256, 1024)

    def tm_step(i, carry):
        k = i // 4
        half = (i // 2) % 2
        cols = pl.ds(pl.multiple_of((i % 2) * 256, 256), 256)
        tmat[k, pl.ds(pl.multiple_of(half * 256, 256), 256), cols] = (
            dot(x_rows(0, half), st[k, 0:1024, cols]) + dot(x_rows(1, half), st[k, 1024:2048, cols])
        )
        return carry

    def gx_step(i, carry):
        r, t = i // 2, i % 2
        value = dot_nt(x_rows(0, r), x_rows(0, t)) + dot_nt(x_rows(1, r), x_rows(1, t))
        rows = pl.ds(pl.multiple_of(r * 256, 256), 256)
        cols = pl.ds(pl.multiple_of(t * 256, 256), 256)
        high = value.astype(BF16)
        gx[0, rows, cols] = high
        gx[1, rows, cols] = (value - high.astype(F32)).astype(BF16)
        return carry

    xo = pltpu.make_async_copy(xg, x_out, lsem.at[7])
    xo.start()

    def grad_step(s, i):
        p, half, n = i // 4, (i // 2) % 2, i % 2
        rows = pl.ds(pl.multiple_of(n * 256, 256), 256)
        value = dot_nt(rp[s, 0, p, half].reshape(256, W), down_w[rows, s * W:s * W + W])
        value = value + dot_nt(
            rp[s, 1, p, half].reshape(256, W), down_w[rows, 1024 + s * W:1024 + s * W + W]
        )
        if s > 0:
            value = value + gacc[p, half, :, rows]
        gacc[p, half, :, rows] = value

    def grad(s):
        def step(i, carry):
            grad_step(s, i)
            return carry

        lax.fori_loop(0, 8, step, 0)

    def all_sum(stat, slot_y, slot_x):
        mine = (yh * 2 + yl) * 2 + c
        slot_y[mine] = stat[...]
        ref = slot_y.at[mine]
        first = go_sent(*[remote(ref, ref, who) for who in p_yc])
        yield
        for copy in first:
            copy.wait_recv()
        total = slot_y[0]
        for i in range(1, 8):
            total = total + slot_y[i]
        here = x * 4 + z
        slot_x[here] = total
        ref = slot_x.at[here]
        second = go_sent(*[remote(ref, ref, who) for who in p_xz])
        yield
        for copy in second:
            copy.wait_recv()
        total = slot_x[0]
        for i in range(1, 16):
            total = total + slot_x[i]
        yield jnp.sum(total, axis=1, keepdims=True) * (1.0 / (D * FF))

    def gram_range(first, last, accs):
        def step(i, accs):
            row = pl.multiple_of(i * 16, 16)
            accs = list(accs)
            for col in range(4):
                v = [
                    st[k, pl.ds(row, 16), col * 128:(col + 1) * 128].astype(F32)
                    for k in range(STORED)
                ]
                for n, (j, k) in enumerate(PAIRS):
                    prod = v[j] * v[k]
                    accs[n] = accs[n] + prod[0:8] + prod[8:16]
            return tuple(accs)

        return lax.fori_loop(first, last, step, accs)

    accs = tuple(jnp.zeros((8, 128), F32) for _ in PAIRS)
    stages = (c2_issue, c3_issue, d1_issue, d2_issue, d3_issue, d4_issue)
    for turn in range(1, S + 7):
        for n, stage in enumerate(stages):
            if 0 <= turn - 1 - n < S:
                stage(turn - 1 - n)
        if turn + 1 < S:
            c1_issue(turn + 1)
        if turn == 1:
            for copy in ab1:
                copy.wait_recv()
            ref = ab.at[:, qy]
            ab2 = go_sent(remote(ref, ref, p_core))
        if turn <= 4:
            lax.fori_loop(6 * turn - 6, 6 * turn, tm_step, 0)
        if turn == 4:
            lax.fori_loop(0, 4, gx_step, 0)
        if 5 <= turn < 9:
            accs = gram_range(32 * turn - 160, 32 * turn - 128, accs)
        if turn == 8:
            for n in range(N_GRAM):
                stat_g[n:n + 1, :] = jnp.sum(accs[n], axis=0, keepdims=True)
            stat_g[N_GRAM:32, :] = jnp.zeros((32 - N_GRAM, 128), F32)
            gram_sum = all_sum(stat_g, slot_gy, slot_gx)
            next(gram_sum)
        if turn == 9:
            next(gram_sum)
        s = turn - 7
        if 0 <= s < S:
            for copy in d4[s]:
                copy.wait_recv()
            if s < S - 1:
                grad(s)
    ab2[0].wait_recv()

    def last_grad(half):
        def step(i, carry):
            p, n = i // 2, i % 2
            grad_step(S - 1, p * 4 + half * 2 + n)
            return carry

        lax.fori_loop(0, 4, step, 0)
        for i in range(2):
            b_q, a_q = ab[1, half * 2 + i], ab[0, half * 2 + i]
            rows = slice(i * 128, i * 128 + 128)
            pa[half, rows, :] = gacc[1, half, rows, :] * a_q + gacc[0, half, rows, :] * b_q

    last_grad(1 - c)
    e1 = go_sent(remote(pa.at[1 - c], rg, p_core))
    last_grad(c)
    own = pl.ds(pl.multiple_of(yl * 128, 128), 128)
    other = pl.ds(pl.multiple_of((1 - yl) * 128, 128), 128)
    e1[0].wait_recv()
    sy[...] = (pa[c, other, :] + rg[other, :]).astype(E_Y)
    e2 = go_sent(remote(sy, ry, p_yl))
    e2[0].wait_recv()
    adj[q] = (pa[c, own, :] + rg[own, :] + ry[...].astype(F32)).astype(BF16)
    e3 = go_sent(
        remote(adj.at[q], adj.at[q], p_yl),
        remote(adj.at[q], adj.at[q], p_core),
    )
    means = next(gram_sum)
    gram = {}
    for n, (j, k) in enumerate(PAIRS):
        gram[j, k] = gram[k, j] = means[n:n + 1, :]
    lower = {}
    inverse = []
    for j in range(STORED):
        pivot = gram[j, j]
        for n in range(j):
            pivot = pivot - lower[j, n] * lower[j, n]
        pivot = jnp.sqrt(pivot)
        inverse.append(1.0 / pivot)
        for i in range(j + 1, STORED):
            entry = gram[i, j]
            for n in range(j):
                entry = entry - lower[i, n] * lower[j, n]
            lower[i, j] = entry * inverse[j]
    e3[0].wait_recv()
    e4 = go_sent(remote(adj.at[qy], adj.at[qy], p_core))
    e3[1].wait_recv()
    e4[0].wait_recv()
    ao = pltpu.make_async_copy(adj, adj_out, lsem.at[8])
    ao.start()

    for k in range(STORED):
        total = jnp.zeros((1, 128), F32)
        for i in range(4):
            right = adj[i].astype(F32)
            if k == 6:
                for j in range(J):
                    left = part[j, 2, i // 2, (i % 2) * 2:(i % 2) * 2 + 2].reshape(128, 256)
                    total = total + fold(left * right[:, j * 256:j * 256 + 256])
            else:
                total = total + fold(tmat[k, i * 128:i * 128 + 128, :] * right)
        stat_c[k:k + 1, :] = total
    whole = adj[...].reshape(512, 512)
    total = jnp.zeros((1, 128), F32)
    for i in range(2):
        rows = slice(i * 256, i * 256 + 256)
        mixed = dot(gx[0, rows, :], whole) + dot(gx[1, rows, :], whole)
        total = total + fold(mixed * whole[i * 256:i * 256 + 256].astype(F32))
    stat_c[7:8, :] = total

    corr_sum = all_sum(stat_c, slot_cy, slot_cx)
    next(corr_sum)
    next(corr_sum)
    means = next(corr_sum)
    corr = [means[n:n + 1, :] for n in range(STORED)]
    power = means[7:8, :]
    forward = []
    for j in range(STORED):
        running = corr[j]
        for n in range(j):
            running = running - lower[j, n] * forward[n]
        forward.append(running * inverse[j])
    load = [None] * STORED
    for j in reversed(range(STORED)):
        running = forward[j]
        for n in range(j + 1, STORED):
            running = running - lower[n, j] * load[n]
        load[j] = running * inverse[j]
    rest = power
    for j in range(STORED):
        inner = -2.0 * corr[j]
        for k in range(STORED):
            inner = inner + gram[j, k] * load[k]
        rest = rest + load[j] * inner
    rest = jnp.maximum(rest, 0.0)
    scale = 1.0 / jnp.sqrt(rest + 1e-06)
    share = jnp.sqrt((rest + 1e-06) / (power + 1e-06))
    rows = [-(load[j] * scale) for j in range(STORED)] + [scale, share]
    rows = rows + [jnp.zeros((1, 1), F32)] * (16 - len(rows))
    for n in range(16):
        coef_out[n:n + 1, :] = jnp.broadcast_to(rows[n], (1, 128))

    for copy in sent:
        copy.wait_send()
    xo.wait()
    ao.wait()


def final_kernel(coef, x_ref, adj_ref, st_ref, out_ref, share_ref):
    @pl.when(pl.program_id(0) == 0)
    def _():
        share_ref[0] = coef[8, 0]

    left = x_ref[0].reshape(512, x_ref.shape[-1])
    image = lax.dot_general(
        left, adj_ref[...], (((0,), (0,)), ((), ())), preferred_element_type=F32
    )
    total = image * coef[7, 0]
    for k in range(STORED):
        total = total + coef[k, 0] * st_ref[k].astype(F32)
    out_ref[...] = total


def body(inputs, targets, gate_weight, up_weight, down_weight, stored_vectors):
    any_spec = pl.BlockSpec(memory_space=pl.ANY)
    n_copies = 220
    adj, xg, coef = pl.pallas_call(
        comm_kernel,
        out_shape=(
            jax.ShapeDtypeStruct((4, 128, 512), BF16),
            jax.ShapeDtypeStruct((2, 2, 4, 4, 16, 1024), BF16),
            jax.ShapeDtypeStruct((16, 128), F32),
        ),
        in_specs=[any_spec] * 6,
        out_specs=(any_spec, any_spec, pl.BlockSpec(memory_space=pltpu.VMEM)),
        scratch_shapes=[
            pltpu.VMEM((2, 2, 4, 4, 16, 1024), BF16),
            pltpu.VMEM((16, 2048), BF16),
            pltpu.VMEM((2048, 512), BF16),
            pltpu.VMEM((2048, 512), BF16),
            pltpu.VMEM((512, 2048), BF16),
            pltpu.VMEM((STORED, 2048, 512), BF16),
            pltpu.VMEM((J, 3, 2, 4, 4, 16, 256), F32),
            pltpu.VMEM((J, 3, 4, 4, 16, 256), F32),
            pltpu.VMEM((J, 3, 2, 4, 16, 256), B_Y),
            pltpu.VMEM((J, 3, 2, 4, 16, 256), B_Y),
            pltpu.VMEM((STORED - 1, 512, 512), F32),
            pltpu.VMEM((2, 512, 512), BF16),
            pltpu.VMEM((J, 2, 4, 128, 256), BF16),
            pltpu.VMEM((2, 4, 128, 512), F32),
            pltpu.VMEM((S, 2, 4, 4, 4, 16, W), C1),
            pltpu.VMEM((S, 2, 3, 4, 4, 16, W), C1),
            pltpu.VMEM((S, 2, 2, 4, 16, W), C2),
            pltpu.VMEM((S, 2, 2, 4, 16, W), F32),
            pltpu.VMEM((S, 2, 2, 4, 16, W), C2),
            pltpu.VMEM((S, 2, 2, 4, 16, W), C3),
            pltpu.VMEM((S, 2, 2, 4, 16, W), F32),
            pltpu.VMEM((S, 2, 3, 2, 16, W), C3),
            pltpu.VMEM((S, 2, 2, 2, 4, 4, 16, W), BF16),
            pltpu.VMEM((2, 2, 256, 512), F32),
            pltpu.VMEM((2, 256, 512), F32),
            pltpu.VMEM((256, 512), F32),
            pltpu.VMEM((128, 512), E_Y),
            pltpu.VMEM((128, 512), E_Y),
            pltpu.VMEM((4, 128, 512), BF16),
            pltpu.VMEM((32, 128), F32),
            pltpu.VMEM((8, 32, 128), F32),
            pltpu.VMEM((16, 32, 128), F32),
            pltpu.VMEM((8, 128), F32),
            pltpu.VMEM((8, 8, 128), F32),
            pltpu.VMEM((16, 8, 128), F32),
            pltpu.SemaphoreType.DMA((9,)),
            pltpu.SemaphoreType.DMA((n_copies,)),
            pltpu.SemaphoreType.DMA((n_copies,)),
        ],
        compiler_params=pltpu.CompilerParams(
            collective_id=0, has_side_effects=True, vmem_limit_bytes=62 * 2**20
        ),
        name="exchange",
    )(inputs, targets, gate_weight, up_weight, down_weight, stored_vectors)

    tile = 256
    per_half = 1024 // tile
    next_vector, share = pl.pallas_call(
        final_kernel,
        grid=(2048 // tile,),
        out_shape=(
            jax.ShapeDtypeStruct((2048, 512), F32),
            jax.ShapeDtypeStruct((1,), F32),
        ),
        in_specs=[
            pl.BlockSpec(memory_space=pltpu.SMEM),
            pl.BlockSpec((1, 512, tile), lambda i: (i // per_half, 0, i % per_half)),
            pl.BlockSpec((512, 512), lambda i: (0, 0)),
            pl.BlockSpec((STORED, tile, 512), lambda i: (0, i, 0)),
        ],
        out_specs=(
            pl.BlockSpec((tile, 512), lambda i: (i, 0)),
            pl.BlockSpec(memory_space=pltpu.SMEM),
        ),
        compiler_params=pltpu.CompilerParams(vmem_limit_bytes=60 * 2**20),
        name="finish",
    )(coef, xg.reshape(2, 512, 1024), adj.reshape(512, 512), stored_vectors)
    return next_vector, share


def solution(mesh):
    return jax.shard_map(
        body,
        mesh=mesh,
        in_specs=(
            P("ffn", "mp"),
            P("ffn", "mp"),
            P("mp", "ffn"),
            P("mp", "ffn"),
            P("ffn", "mp"),
            P(None, "mp", "ffn"),
        ),
        out_specs=(P("mp", "ffn"), P()),
        check_vma=False,
    )
```

```python
import functools

import jax
import jax.numpy as jnp
from jax import lax
from jax.experimental import pallas as pl
from jax.experimental.pallas import tpu as pltpu
from jax.sharding import PartitionSpec as P

D = 8192
FF = 16384
STORED = 7
MESH = pl.DeviceIdType.MESH
F32 = jnp.float32
BF16 = jnp.bfloat16
PAIRS = [(j, k) for j in range(STORED) for k in range(j, STORED)]
N_GRAM = len(PAIRS)

B_Y = BF16
C1 = BF16
C2 = BF16
C3 = BF16
E_Y = BF16
S = 4
W = 256


def dot(left, right):
    return jnp.dot(left, right, preferred_element_type=F32)


def dot_nt(left, right):
    return lax.dot_general(left, right, (((1,), (1,)), ((), ())), preferred_element_type=F32)


def fold(values):
    rows, lanes = values.shape
    part = jnp.sum(values.reshape(rows // 8, 8, lanes), axis=0)
    total = part[:, 0:128]
    for n in range(1, lanes // 128):
        total = total + part[:, n * 128:n * 128 + 128]
    return jnp.sum(total, axis=0, keepdims=True)


def comm_kernel(
    x_hbm, tgt_hbm, gate_hbm, up_hbm, down_hbm, stored_hbm,
    adj_out, x_out, coef_out,
    xg, tgt, gate_w, up_w, down_w, st,
    part, rb, sby, rby, tmat, gx,
    hp, ab, s1, r1, s2, s2_own, r2, s3, s3_own, r3, rp,
    gacc, pa, rg, sy, ry, adj,
    stat_g, slot_gy, slot_gx, stat_c, slot_cy, slot_cx,
    lsem, ssem, rsem,
):
    f = lax.axis_index("ffn")
    m = lax.axis_index("mp")
    yh, x, z = f // 16, (f // 4) % 4, f % 4
    yl, c = m // 2, m % 2
    q = c * 2 + yl
    qy = c * 2 + (1 - yl)

    def at(yh_=yh, x_=x, z_=z, yl_=yl, c_=c):
        return (yh_ * 16 + x_ * 4 + z_, yl_ * 2 + c_)

    xs = [(x + d) % 4 for d in (1, 3, 2)]
    zs = [(z + d) % 4 for d in (1, 3, 2)]
    p_x = [at(x_=v) for v in xs]
    p_z = [at(z_=v) for v in zs]
    p_yc = [
        at(yh_=(yh + i) % 2, yl_=(yl + j) % 2, c_=(c + k) % 2)
        for i in range(2) for j in range(2) for k in range(2) if i + j + k > 0
    ]
    p_xz = [
        at(x_=(x + i) % 4, z_=(z + j) % 4) for i in range(4) for j in range(4) if i + j > 0
    ]
    p_core, p_yl, p_yh = at(c_=1 - c), at(yl_=1 - yl), at(yh_=1 - yh)
    peers = [p_core, p_yl, p_yh] + p_x + p_z

    counter = [0]

    def remote(src, dst, who):
        i = counter[0]
        counter[0] += 1
        return pltpu.make_async_remote_copy(
            src_ref=src, dst_ref=dst, send_sem=ssem.at[i], recv_sem=rsem.at[i],
            device_id=who, device_id_type=MESH,
        )

    sent = []

    def go(*copies):
        for copy in copies:
            copy.start()
        return list(copies)

    def go_sent(*copies):
        sent.extend(go(*copies))
        return list(copies)

    loads = [
        pltpu.make_async_copy(x_hbm.at[:, pl.ds(h * 1024, 1024)], xg.at[h, yh, x, z], lsem.at[h])
        for h in range(2)
    ]
    late = [
        pltpu.make_async_copy(gate_hbm, gate_w, lsem.at[2]),
        pltpu.make_async_copy(up_hbm, up_w, lsem.at[3]),
        pltpu.make_async_copy(stored_hbm, st, lsem.at[4]),
        pltpu.make_async_copy(down_hbm, down_w, lsem.at[5]),
        pltpu.make_async_copy(tgt_hbm, tgt.at[yh], lsem.at[6]),
    ]
    go(*loads)
    go(*late)

    barrier = pltpu.get_barrier_semaphore()
    for who in peers:
        pl.semaphore_signal(barrier, inc=1, device_id=who, device_id_type=MESH)
    for t in range(2):
        for n in range(3):
            part[t, n] = jnp.zeros(part.shape[2:], F32)
    pl.semaphore_wait(barrier, len(peers))
    for copy in loads:
        copy.wait()

    def block(h, yh_):
        return xg.at[h, yh_, x, z]

    a1 = go_sent(remote(xg.at[:, yh, x, z], xg.at[:, yh, x, z], p_yh))
    a2 = {}
    a3 = {}

    def second(i, w):
        a2[i] = []
        for d in range(3):
            a2[i] += go_sent(
                remote(block(0, w), block(0, w), p_z[d]),
                remote(block(1, w), block(1, w), p_x[d]),
            )

    def third(t):
        a3[t] = []
        for d in range(3):
            a3[t] += go_sent(
                remote(xg.at[0, t, x], xg.at[0, t, x], p_x[d]),
                remote(xg.at[1, t, :, z], xg.at[1, t, :, z], p_z[d]),
            )

    second(0, yh)
    a1[0].wait_recv()
    second(1, 1 - yh)
    for i in range(2):
        for copy in a2[i]:
            copy.wait_recv()
    third(0)
    third(1)
    for copy in late:
        copy.wait()
    goal = go_sent(remote(tgt.at[yh], tgt.at[yh], p_yh))

    def partial(t, h, lines):
        def step(j, carry):
            cols = pl.ds(pl.multiple_of(j * 256, 256), 256)
            left = jnp.concatenate(
                [(xg[0, t, l] if h == 0 else xg[1, t, :, l]).reshape(64, 1024) for l in lines], axis=0
            )
            depth = slice(h * 1024, h * 1024 + 1024)
            for n in range(3):
                right = (gate_w, up_w)[n][depth, cols] if n < 2 else st[6, depth, cols]
                value = dot(left, right)
                for i, l in enumerate(lines):
                    piece = value[i * 64:i * 64 + 64].reshape(4, 16, 256)
                    if h == 0:
                        part[t, n, l, :, :, cols] = part[t, n, l, :, :, cols] + piece
                    else:
                        part[t, n, :, l, :, cols] = part[t, n, :, l, :, cols] + piece
            return carry

        lax.fori_loop(0, 2, step, 0)

    def partials(t):
        a3[t][0].wait_recv()
        partial(t, 0, (x, xs[1]))
        a3[t][1].wait_recv()
        partial(t, 1, (z, zs[1]))
        a3[t][2].wait_recv()
        a3[t][4].wait_recv()
        partial(t, 0, (xs[0], xs[2]))
        a3[t][3].wait_recv()
        a3[t][5].wait_recv()
        partial(t, 1, (zs[0], zs[2]))

    b1, b2, b3, b4 = {}, {}, {}, {}

    def b_core(t):
        b1[t] = go_sent(remote(part.at[t, :, pl.ds((1 - c) * 2, 2)], rb.at[t], p_core))

    def b_y(t):
        b1[t][0].wait_recv()
        for n in range(3):
            sby[t, n] = (part[t, n, qy] + rb[t, n, 1 - yl]).astype(B_Y)
        b2[t] = go_sent(remote(sby.at[t], rby.at[t], p_yl))

    def b_hidden(t):
        b2[t][0].wait_recv()
        gate, upv, tang = [
            (part[t, n, q] + rb[t, n, yl] + rby[t, n].astype(F32)).reshape(64, 512)
            for n in range(3)
        ]
        sg = 1.0 / (1.0 + jnp.exp(-gate))
        swish = gate * sg
        slope = sg * (1.0 + gate * (1.0 - sg))
        curve = sg * (1.0 - sg) * (2.0 + gate * (1.0 - 2.0 * sg))
        hp[t, 0, q] = (swish * upv).astype(BF16)
        hp[t, 1, q] = (slope * upv * tang).astype(BF16)
        ref = hp.at[t, :, q]
        b3[t] = go_sent(remote(ref, ref, p_yl), remote(ref, ref, p_core))
        ab[t, 0, q] = upv * slope
        ab[t, 1, q] = upv * curve * tang

    def b_forward(t):
        b3[t][0].wait_recv()
        ref = hp.at[t, :, qy]
        b4[t] = go_sent(remote(ref, ref, p_core))

    def b_done(t):
        b3[t][1].wait_recv()
        b4[t][0].wait_recv()

    c1, c2, c3, d1, d2, d3, d4 = {}, {}, {}, {}, {}, {}, {}

    def first_col(s, h, u):
        return h * 1024 + u * 512 + (s % 2) * W

    def c1_issue(s):
        c1[s] = []
        t = s // 2
        for u in range(2):
            for r in range(4):
                p, h = r // 2, r % 2
                col = first_col(s, h, u)
                value = dot(hp[t, p].reshape(256, 512), down_w[:, col:col + W])
                s1[s, u, r] = value.astype(C1).reshape(4, 4, 16, W)
            for d in range(3):
                if u == 0:
                    c1[s] += go_sent(remote(s1.at[s, 0, :, :, zs[d]], r1.at[s, 0, d], p_z[d]))
                else:
                    c1[s] += go_sent(remote(s1.at[s, 1, :, xs[d]], r1.at[s, 1, d], p_x[d]))

    def c2_issue(s):
        for h in range(2):
            for d in range(3):
                c1[s][h * 3 + d].wait_recv()

            def sum_step(i, carry, h=h):
                p, g = i // 4, i % 4
                for own in range(2):
                    w = yh if own else 1 - yh
                    r = p * 2 + w
                    here = s1[s, 0, r, g, z] if h == 0 else s1[s, 1, r, x, g]
                    total = here.astype(F32)
                    for d in range(3):
                        total = total + r1[s, h, d, r, g].astype(F32)
                    if own:
                        s2_own[s, h, p, g] = total
                    else:
                        s2[s, h, p, g] = total.astype(C2)
                return carry

            lax.fori_loop(0, 8, sum_step, 0)
        c2[s] = go_sent(remote(s2.at[s], r2.at[s], p_yh))

    def c3_issue(s):
        c2[s][0].wait_recv()
        c3[s] = []
        for h in range(2):
            for p in range(2):
                total = s2_own[s, h, p] + r2[s, h, p].astype(F32)
                s3_own[s, h, p] = total
                s3[s, h, p] = total.astype(C3)
            for d in range(3):
                if h == 0:
                    c3[s] += go_sent(remote(s3.at[s, 0, :, xs[d]], r3.at[s, 0, d], p_x[d]))
                else:
                    c3[s] += go_sent(remote(s3.at[s, 1, :, zs[d]], r3.at[s, 1, d], p_z[d]))

    def d1_issue(s):
        for copy in c3[s]:
            copy.wait_recv()
        d1[s] = []
        for h in range(2):
            for p in range(2):
                total = s3_own[s, h, p, x if h == 0 else z]
                for d in range(3):
                    total = total + r3[s, h, d, p].astype(F32)
                if p == 0:
                    wide = pl.ds(pl.multiple_of(first_col(s, yh, h), W), W)
                    total = total - tgt[s // 2, :, wide].astype(F32)
                rp[s, h, p, yh, x, z] = total.astype(BF16)
            ref = rp.at[s, h, :, yh, x, z]
            for d in range(3):
                d1[s] += go_sent(remote(ref, ref, (p_x, p_z)[h][d]))

    def d2_issue(s):
        for copy in d1[s]:
            copy.wait_recv()
        ref0, ref1 = rp.at[s, 0, :, yh, :, z], rp.at[s, 1, :, yh, x]
        d2[s] = go_sent(remote(ref0, ref0, p_yh), remote(ref1, ref1, p_yh))

    def d3_issue(s):
        for copy in d2[s]:
            copy.wait_recv()
        d3[s] = []
        for d in range(2):
            ref0, ref1 = rp.at[s, 0, :, :, :, z], rp.at[s, 1, :, :, x]
            d3[s] += go_sent(remote(ref0, ref0, p_z[d]), remote(ref1, ref1, p_x[d]))

    def d4_issue(s):
        d4[s] = []
        for d in range(2):
            d3[s][2 * d].wait_recv()
            ref = rp.at[s, 0, d, :, :, zs[1 - d]]
            d4[s] += go_sent(remote(ref, ref, p_z[d]))
            d3[s][2 * d + 1].wait_recv()
            ref = rp.at[s, 1, d, :, xs[1 - d]]
            d4[s] += go_sent(remote(ref, ref, p_x[d]))

    partials(0)
    b_core(0)
    b_y(0)
    partials(1)
    b_core(1)
    b_hidden(0)
    b_y(1)
    b_forward(0)
    b_done(0)
    c1_issue(0)
    c1_issue(1)
    b_hidden(1)
    b_forward(1)
    ab1 = []
    for t in range(2):
        ref = ab.at[t, :, q]
        ab1 += go_sent(remote(ref, ref, p_yl), remote(ref, ref, p_core))
    b_done(1)
    goal[0].wait_recv()

    def x_rows(h, half):
        return xg[h, half].reshape(256, 1024)

    def tm_step(i, carry):
        k = i // 4
        half = (i // 2) % 2
        cols = pl.ds(pl.multiple_of((i % 2) * 256, 256), 256)
        tmat[k, pl.ds(pl.multiple_of(half * 256, 256), 256), cols] = (
            dot(x_rows(0, half), st[k, 0:1024, cols]) + dot(x_rows(1, half), st[k, 1024:2048, cols])
        )
        return carry

    def gx_step(i, carry):
        r, t = i // 2, i % 2
        value = dot_nt(x_rows(0, r), x_rows(0, t)) + dot_nt(x_rows(1, r), x_rows(1, t))
        rows = pl.ds(pl.multiple_of(r * 256, 256), 256)
        cols = pl.ds(pl.multiple_of(t * 256, 256), 256)
        high = value.astype(BF16)
        gx[0, rows, cols] = high
        gx[1, rows, cols] = (value - high.astype(F32)).astype(BF16)
        return carry

    xo = pltpu.make_async_copy(xg, x_out, lsem.at[7])
    xo.start()

    def grad(s):
        t = s // 2
        for p in range(2):
            def step(n, carry, p=p):
                rows = pl.ds(pl.multiple_of(n * 256, 256), 256)
                value = jnp.zeros((256, 256), F32)
                for u in range(2):
                    for h in range(2):
                        col = first_col(s, h, u)
                        value = value + dot_nt(rp[s, u, p, h].reshape(256, W), down_w[rows, col:col + W])
                if s % 2:
                    value = value + gacc[t, p, :, rows]
                gacc[t, p, :, rows] = value
                return carry

            lax.fori_loop(0, 2, step, 0)

    e1, e2, e3, e4 = {}, {}, {}, {}

    def e_core(t):
        for i in range(4):
            rows = slice(i * 64, i * 64 + 64)
            pa[t, i] = gacc[t, 1, rows, :] * ab[t, 0, i] + gacc[t, 0, rows, :] * ab[t, 1, i]
        e1[t] = go_sent(remote(pa.at[t, pl.ds((1 - c) * 2, 2)], rg.at[t], p_core))

    def e_y(t):
        e1[t][0].wait_recv()
        sy[t] = (pa[t, qy] + rg[t, 1 - yl]).astype(E_Y)
        e2[t] = go_sent(remote(sy.at[t], ry.at[t], p_yl))

    def e_adjoint(t):
        e2[t][0].wait_recv()
        adj[t, q] = (pa[t, q] + rg[t, yl] + ry[t].astype(F32)).astype(BF16)
        ref = adj.at[t, q]
        e3[t] = go_sent(remote(ref, ref, p_yl), remote(ref, ref, p_core))

    def e_forward(t):
        e3[t][0].wait_recv()
        e4[t] = go_sent(remote(adj.at[t, qy], adj.at[t, qy], p_core))

    def e_done(t):
        e3[t][1].wait_recv()
        e4[t][0].wait_recv()

    def correlate(t):
        for k in range(STORED):
            total = jnp.zeros((1, 128), F32) if t == 0 else stat_c[k:k + 1, :]
            for i in range(2):
                right = adj[t, 2 * i:2 * i + 2].reshape(128, 512).astype(F32)
                if k == 6:
                    left = part[t, 2, 2 * i:2 * i + 2].reshape(128, 512)
                else:
                    left = tmat[k, t * 256 + i * 128:t * 256 + i * 128 + 128, :]
                total = total + fold(left * right)
            stat_c[k:k + 1, :] = total

    def all_sum(stat, slot_y, slot_x):
        mine = (yh * 2 + yl) * 2 + c
        slot_y[mine] = stat[...]
        ref = slot_y.at[mine]
        first = go_sent(*[remote(ref, ref, who) for who in p_yc])
        yield
        for copy in first:
            copy.wait_recv()
        total = slot_y[0]
        for i in range(1, 8):
            total = total + slot_y[i]
        here = x * 4 + z
        slot_x[here] = total
        ref = slot_x.at[here]
        second = go_sent(*[remote(ref, ref, who) for who in p_xz])
        yield
        for copy in second:
            copy.wait_recv()
        total = slot_x[0]
        for i in range(1, 16):
            total = total + slot_x[i]
        yield jnp.sum(total, axis=1, keepdims=True) * (1.0 / (D * FF))

    def gram_range(first, last, accs):
        def step(i, accs):
            row = pl.multiple_of(i * 16, 16)
            accs = list(accs)
            for col in range(4):
                v = [
                    st[k, pl.ds(row, 16), col * 128:(col + 1) * 128].astype(F32)
                    for k in range(STORED)
                ]
                for n, (j, k) in enumerate(PAIRS):
                    prod = v[j] * v[k]
                    accs[n] = accs[n] + prod[0:8] + prod[8:16]
            return tuple(accs)

        return lax.fori_loop(first, last, step, accs)

    accs = tuple(jnp.zeros((8, 128), F32) for _ in PAIRS)
    stages = (c2_issue, c3_issue, d1_issue, d2_issue, d3_issue, d4_issue)
    for turn in range(1, S + 7):
        for n, stage in enumerate(stages):
            if 0 <= turn - 1 - n < S:
                stage(turn - 1 - n)
        if turn + 1 < S:
            c1_issue(turn + 1)
        if turn == 1:
            for copy in ab1:
                copy.wait_recv()
            ref = ab.at[:, :, qy]
            ab2 = go_sent(remote(ref, ref, p_core))
        if turn <= 4:
            lax.fori_loop(6 * turn - 6, 6 * turn, tm_step, 0)
        if turn == 4:
            lax.fori_loop(0, 4, gx_step, 0)
        if 5 <= turn < 9:
            accs = gram_range(32 * turn - 160, 32 * turn - 128, accs)
        if turn == 8:
            for n in range(N_GRAM):
                stat_g[n:n + 1, :] = jnp.sum(accs[n], axis=0, keepdims=True)
            stat_g[N_GRAM:32, :] = jnp.zeros((32 - N_GRAM, 128), F32)
            gram_sum = all_sum(stat_g, slot_gy, slot_gx)
            next(gram_sum)
        if turn == 9:
            next(gram_sum)
        if turn == 9:
            e_y(0)
        if turn == 10:
            e_adjoint(0)
        s = turn - 7
        if 0 <= s < S:
            for copy in d4[s]:
                copy.wait_recv()
            grad(s)
            if s == 0:
                ab2[0].wait_recv()
            if s % 2:
                e_core(s // 2)
    e_forward(0)
    e_y(1)
    e_done(0)
    correlate(0)
    e_adjoint(1)
    means = next(gram_sum)
    gram = {}
    for n, (j, k) in enumerate(PAIRS):
        gram[j, k] = gram[k, j] = means[n:n + 1, :]
    lower = {}
    inverse = []
    for j in range(STORED):
        pivot = gram[j, j]
        for n in range(j):
            pivot = pivot - lower[j, n] * lower[j, n]
        pivot = jnp.sqrt(pivot)
        inverse.append(1.0 / pivot)
        for i in range(j + 1, STORED):
            entry = gram[i, j]
            for n in range(j):
                entry = entry - lower[i, n] * lower[j, n]
            lower[i, j] = entry * inverse[j]
    e_forward(1)
    e_done(1)
    ao = pltpu.make_async_copy(adj, adj_out, lsem.at[8])
    ao.start()

    correlate(1)
    whole = adj[...].reshape(512, 512)
    total = jnp.zeros((1, 128), F32)
    for i in range(2):
        rows = slice(i * 256, i * 256 + 256)
        mixed = dot(gx[0, rows, :], whole) + dot(gx[1, rows, :], whole)
        total = total + fold(mixed * whole[i * 256:i * 256 + 256].astype(F32))
    stat_c[7:8, :] = total

    corr_sum = all_sum(stat_c, slot_cy, slot_cx)
    next(corr_sum)
    next(corr_sum)
    means = next(corr_sum)
    corr = [means[n:n + 1, :] for n in range(STORED)]
    power = means[7:8, :]
    forward = []
    for j in range(STORED):
        running = corr[j]
        for n in range(j):
            running = running - lower[j, n] * forward[n]
        forward.append(running * inverse[j])
    load = [None] * STORED
    for j in reversed(range(STORED)):
        running = forward[j]
        for n in range(j + 1, STORED):
            running = running - lower[n, j] * load[n]
        load[j] = running * inverse[j]
    rest = power
    for j in range(STORED):
        inner = -2.0 * corr[j]
        for k in range(STORED):
            inner = inner + gram[j, k] * load[k]
        rest = rest + load[j] * inner
    rest = jnp.maximum(rest, 0.0)
    scale = 1.0 / jnp.sqrt(rest + 1e-06)
    share = jnp.sqrt((rest + 1e-06) / (power + 1e-06))
    rows = [-(load[j] * scale) for j in range(STORED)] + [scale, share]
    rows = rows + [jnp.zeros((1, 1), F32)] * (16 - len(rows))
    for n in range(16):
        coef_out[n:n + 1, :] = jnp.broadcast_to(rows[n], (1, 128))

    for copy in sent:
        copy.wait_send()
    xo.wait()
    ao.wait()


def final_kernel(coef, x_ref, adj_ref, st_ref, out_ref, share_ref):
    @pl.when(pl.program_id(0) == 0)
    def _():
        share_ref[0] = coef[8, 0]

    left = x_ref[0].reshape(512, x_ref.shape[-1])
    image = lax.dot_general(
        left, adj_ref[...], (((0,), (0,)), ((), ())), preferred_element_type=F32
    )
    total = image * coef[7, 0]
    for k in range(STORED):
        total = total + coef[k, 0] * st_ref[k].astype(F32)
    out_ref[...] = total


def body(inputs, targets, gate_weight, up_weight, down_weight, stored_vectors):
    any_spec = pl.BlockSpec(memory_space=pl.ANY)
    n_copies = 220
    adj, xg, coef = pl.pallas_call(
        comm_kernel,
        out_shape=(
            jax.ShapeDtypeStruct((2, 4, 64, 512), BF16),
            jax.ShapeDtypeStruct((2, 2, 4, 4, 16, 1024), BF16),
            jax.ShapeDtypeStruct((16, 128), F32),
        ),
        in_specs=[any_spec] * 6,
        out_specs=(any_spec, any_spec, pl.BlockSpec(memory_space=pltpu.VMEM)),
        scratch_shapes=[
            pltpu.VMEM((2, 2, 4, 4, 16, 1024), BF16),
            pltpu.VMEM((2, 16, 2048), BF16),
            pltpu.VMEM((2048, 512), BF16),
            pltpu.VMEM((2048, 512), BF16),
            pltpu.VMEM((512, 2048), BF16),
            pltpu.VMEM((STORED, 2048, 512), BF16),
            pltpu.VMEM((2, 3, 4, 4, 16, 512), F32),
            pltpu.VMEM((2, 3, 2, 4, 16, 512), F32),
            pltpu.VMEM((2, 3, 4, 16, 512), B_Y),
            pltpu.VMEM((2, 3, 4, 16, 512), B_Y),
            pltpu.VMEM((STORED - 1, 512, 512), F32),
            pltpu.VMEM((2, 512, 512), BF16),
            pltpu.VMEM((2, 2, 4, 64, 512), BF16),
            pltpu.VMEM((2, 2, 4, 64, 512), F32),
            pltpu.VMEM((S, 2, 4, 4, 4, 16, W), C1),
            pltpu.VMEM((S, 2, 3, 4, 4, 16, W), C1),
            pltpu.VMEM((S, 2, 2, 4, 16, W), C2),
            pltpu.VMEM((S, 2, 2, 4, 16, W), F32),
            pltpu.VMEM((S, 2, 2, 4, 16, W), C2),
            pltpu.VMEM((S, 2, 2, 4, 16, W), C3),
            pltpu.VMEM((S, 2, 2, 4, 16, W), F32),
            pltpu.VMEM((S, 2, 3, 2, 16, W), C3),
            pltpu.VMEM((S, 2, 2, 2, 4, 4, 16, W), BF16),
            pltpu.VMEM((2, 2, 256, 512), F32),
            pltpu.VMEM((2, 4, 64, 512), F32),
            pltpu.VMEM((2, 2, 64, 512), F32),
            pltpu.VMEM((2, 64, 512), E_Y),
            pltpu.VMEM((2, 64, 512), E_Y),
            pltpu.VMEM((2, 4, 64, 512), BF16),
            pltpu.VMEM((32, 128), F32),
            pltpu.VMEM((8, 32, 128), F32),
            pltpu.VMEM((16, 32, 128), F32),
            pltpu.VMEM((8, 128), F32),
            pltpu.VMEM((8, 8, 128), F32),
            pltpu.VMEM((16, 8, 128), F32),
            pltpu.SemaphoreType.DMA((9,)),
            pltpu.SemaphoreType.DMA((n_copies,)),
            pltpu.SemaphoreType.DMA((n_copies,)),
        ],
        compiler_params=pltpu.CompilerParams(
            collective_id=0, has_side_effects=True, vmem_limit_bytes=62 * 2**20
        ),
        name="exchange",
    )(inputs, targets, gate_weight, up_weight, down_weight, stored_vectors)

    tile = 512
    per_half = 1024 // tile
    next_vector, share = pl.pallas_call(
        final_kernel,
        grid=(2048 // tile,),
        out_shape=(
            jax.ShapeDtypeStruct((2048, 512), F32),
            jax.ShapeDtypeStruct((1,), F32),
        ),
        in_specs=[
            pl.BlockSpec(memory_space=pltpu.SMEM),
            pl.BlockSpec((1, 512, tile), lambda i: (i // per_half, 0, i % per_half)),
            pl.BlockSpec((512, 512), lambda i: (0, 0)),
            pl.BlockSpec((STORED, tile, 512), lambda i: (0, i, 0)),
        ],
        out_specs=(
            pl.BlockSpec((tile, 512), lambda i: (i, 0)),
            pl.BlockSpec(memory_space=pltpu.SMEM),
        ),
        compiler_params=pltpu.CompilerParams(vmem_limit_bytes=60 * 2**20),
        name="finish",
    )(coef, xg.reshape(2, 512, 1024), adj.reshape(512, 512), stored_vectors)
    return next_vector, share


def solution(mesh):
    return jax.shard_map(
        body,
        mesh=mesh,
        in_specs=(
            P("ffn", "mp"),
            P("ffn", "mp"),
            P("mp", "ffn"),
            P("mp", "ffn"),
            P("ffn", "mp"),
            P(None, "mp", "ffn"),
        ),
        out_specs=(P("mp", "ffn"), P()),
        check_vma=False,
    )
```

```python
import functools

import jax
import jax.numpy as jnp
from jax import lax
from jax.experimental import pallas as pl
from jax.experimental.pallas import tpu as pltpu
from jax.sharding import PartitionSpec as P

D = 8192
FF = 16384
STORED = 7
MESH = pl.DeviceIdType.MESH
F32 = jnp.float32
BF16 = jnp.bfloat16
PAIRS = [(j, k) for j in range(STORED) for k in range(j, STORED)]
N_GRAM = len(PAIRS)

B_Y = BF16
C1 = BF16
C2 = BF16
C3 = BF16
E_Y = BF16
S = 4
W = 256


def dot(left, right):
    return jnp.dot(left, right, preferred_element_type=F32)


def dot_nt(left, right):
    return lax.dot_general(left, right, (((1,), (1,)), ((), ())), preferred_element_type=F32)


def fold(values):
    rows, lanes = values.shape
    part = jnp.sum(values.reshape(rows // 8, 8, lanes), axis=0)
    total = part[:, 0:128]
    for n in range(1, lanes // 128):
        total = total + part[:, n * 128:n * 128 + 128]
    return jnp.sum(total, axis=0, keepdims=True)


def comm_kernel(
    x_hbm, tgt_hbm, gate_hbm, up_hbm, down_hbm, stored_hbm,
    adj_out, x_out, coef_out,
    xg, tgt, gate_w, up_w, down_w, st,
    part, rb, sby, rby, tmat, gx,
    hp, ab, s1, r1, s2, s2_own, r2, s3, s3_own, r3, rp,
    gacc, pa, rg, sy, ry, adj,
    stat_g, slot_gy, slot_gx, stat_c, slot_cy, slot_cx,
    lsem, ssem, rsem,
):
    f = lax.axis_index("ffn")
    m = lax.axis_index("mp")
    yh, x, z = f // 16, (f // 4) % 4, f % 4
    yl, c = m // 2, m % 2
    q = c * 2 + yl
    qy = c * 2 + (1 - yl)

    def at(yh_=yh, x_=x, z_=z, yl_=yl, c_=c):
        return (yh_ * 16 + x_ * 4 + z_, yl_ * 2 + c_)

    xs = [(x + d) % 4 for d in (1, 3, 2)]
    zs = [(z + d) % 4 for d in (1, 3, 2)]
    p_x = [at(x_=v) for v in xs]
    p_z = [at(z_=v) for v in zs]
    p_yc = [
        at(yh_=(yh + i) % 2, yl_=(yl + j) % 2, c_=(c + k) % 2)
        for i in range(2) for j in range(2) for k in range(2) if i + j + k > 0
    ]
    p_xz = [
        at(x_=(x + i) % 4, z_=(z + j) % 4) for i in range(4) for j in range(4) if i + j > 0
    ]
    p_core, p_yl, p_yh = at(c_=1 - c), at(yl_=1 - yl), at(yh_=1 - yh)
    peers = [p_core, p_yl, p_yh] + p_x + p_z

    counter = [0]

    def remote(src, dst, who):
        i = counter[0]
        counter[0] += 1
        return pltpu.make_async_remote_copy(
            src_ref=src, dst_ref=dst, send_sem=ssem.at[i], recv_sem=rsem.at[i],
            device_id=who, device_id_type=MESH,
        )

    sent = []

    def go(*copies):
        for copy in copies:
            copy.start()
        return list(copies)

    def go_sent(*copies):
        sent.extend(go(*copies))
        return list(copies)

    loads = [
        pltpu.make_async_copy(x_hbm.at[:, pl.ds(h * 1024, 1024)], xg.at[h, yh, x, z], lsem.at[h])
        for h in range(2)
    ]
    late = [
        pltpu.make_async_copy(gate_hbm, gate_w, lsem.at[2]),
        pltpu.make_async_copy(up_hbm, up_w, lsem.at[3]),
        pltpu.make_async_copy(stored_hbm, st, lsem.at[4]),
        pltpu.make_async_copy(down_hbm, down_w, lsem.at[5]),
        pltpu.make_async_copy(tgt_hbm, tgt.at[yh], lsem.at[6]),
    ]
    go(*loads)
    go(*late)

    barrier = pltpu.get_barrier_semaphore()
    for who in peers:
        pl.semaphore_signal(barrier, inc=1, device_id=who, device_id_type=MESH)
    for t in range(2):
        for n in range(3):
            part[t, n] = jnp.zeros(part.shape[2:], F32)
    pl.semaphore_wait(barrier, len(peers))
    for copy in loads:
        copy.wait()

    def block(h, yh_):
        return xg.at[h, yh_, x, z]

    a1 = go_sent(remote(xg.at[:, yh, x, z], xg.at[:, yh, x, z], p_yh))
    a2 = {}
    a3 = {}

    def second(i, w):
        a2[i] = []
        for d in range(3):
            a2[i] += go_sent(
                remote(block(0, w), block(0, w), p_z[d]),
                remote(block(1, w), block(1, w), p_x[d]),
            )

    def third(t):
        a3[t] = []
        for d in range(3):
            a3[t] += go_sent(
                remote(xg.at[0, t, x], xg.at[0, t, x], p_x[d]),
                remote(xg.at[1, t, :, z], xg.at[1, t, :, z], p_z[d]),
            )

    second(0, yh)
    a1[0].wait_recv()
    second(1, 1 - yh)
    for i in range(2):
        for copy in a2[i]:
            copy.wait_recv()
    third(0)
    third(1)
    for copy in late:
        copy.wait()
    goal = go_sent(remote(tgt.at[yh], tgt.at[yh], p_yh))

    def partial(t, h, lines):
        def step(j, carry):
            cols = pl.ds(pl.multiple_of(j * 256, 256), 256)
            left = jnp.concatenate(
                [(xg[0, t, l] if h == 0 else xg[1, t, :, l]).reshape(64, 1024) for l in lines], axis=0
            )
            depth = slice(h * 1024, h * 1024 + 1024)
            for n in range(3):
                right = (gate_w, up_w)[n][depth, cols] if n < 2 else st[6, depth, cols]
                value = dot(left, right)
                for i, l in enumerate(lines):
                    piece = value[i * 64:i * 64 + 64].reshape(4, 16, 256)
                    if h == 0:
                        part[t, n, l, :, :, cols] = part[t, n, l, :, :, cols] + piece
                    else:
                        part[t, n, :, l, :, cols] = part[t, n, :, l, :, cols] + piece
            return carry

        lax.fori_loop(0, 2, step, 0)

    def partials(t):
        a3[t][0].wait_recv()
        partial(t, 0, (x, xs[1]))
        a3[t][1].wait_recv()
        partial(t, 1, (z, zs[1]))
        a3[t][2].wait_recv()
        a3[t][4].wait_recv()
        partial(t, 0, (xs[0], xs[2]))
        a3[t][3].wait_recv()
        a3[t][5].wait_recv()
        partial(t, 1, (zs[0], zs[2]))

    b1, b2, b3, b4 = {}, {}, {}, {}

    def b_core(t):
        b1[t] = go_sent(remote(part.at[t, :, pl.ds((1 - c) * 2, 2)], rb.at[t], p_core))

    def b_y(t):
        b1[t][0].wait_recv()
        for n in range(3):
            sby[t, n] = (part[t, n, qy] + rb[t, n, 1 - yl]).astype(B_Y)
        b2[t] = go_sent(remote(sby.at[t], rby.at[t], p_yl))

    def b_hidden(t):
        b2[t][0].wait_recv()
        gate, upv, tang = [
            (part[t, n, q] + rb[t, n, yl] + rby[t, n].astype(F32)).reshape(64, 512)
            for n in range(3)
        ]
        sg = 1.0 / (1.0 + jnp.exp(-gate))
        swish = gate * sg
        slope = sg * (1.0 + gate * (1.0 - sg))
        curve = sg * (1.0 - sg) * (2.0 + gate * (1.0 - 2.0 * sg))
        hp[t, 0, q] = (swish * upv).astype(BF16)
        hp[t, 1, q] = (slope * upv * tang).astype(BF16)
        ref = hp.at[t, :, q]
        b3[t] = go_sent(remote(ref, ref, p_yl), remote(ref, ref, p_core))
        ab[t, 0, q] = upv * slope
        ab[t, 1, q] = upv * curve * tang

    def b_forward(t):
        b3[t][0].wait_recv()
        ref = hp.at[t, :, qy]
        b4[t] = go_sent(remote(ref, ref, p_core))

    def b_done(t):
        b3[t][1].wait_recv()
        b4[t][0].wait_recv()

    c1, c2, c3, d1, d2, d3, d4 = {}, {}, {}, {}, {}, {}, {}

    def first_col(s, h, u):
        return h * 1024 + u * 512 + (s % 2) * W

    def c1_issue(s):
        c1[s] = []
        t = s // 2
        for u in range(2):
            for r in range(4):
                p, h = r // 2, r % 2
                col = first_col(s, h, u)
                value = dot(hp[t, p].reshape(256, 512), down_w[:, col:col + W])
                s1[s, u, r] = value.astype(C1).reshape(4, 4, 16, W)
            for d in range(3):
                if u == 0:
                    c1[s] += go_sent(remote(s1.at[s, 0, :, :, zs[d]], r1.at[s, 0, d], p_z[d]))
                else:
                    c1[s] += go_sent(remote(s1.at[s, 1, :, xs[d]], r1.at[s, 1, d], p_x[d]))

    def c2_issue(s):
        for h in range(2):
            for d in range(3):
                c1[s][h * 3 + d].wait_recv()

            def sum_step(i, carry, h=h):
                p, g = i // 4, i % 4
                for own in range(2):
                    w = yh if own else 1 - yh
                    r = p * 2 + w
                    here = s1[s, 0, r, g, z] if h == 0 else s1[s, 1, r, x, g]
                    total = here.astype(F32)
                    for d in range(3):
                        total = total + r1[s, h, d, r, g].astype(F32)
                    if own:
                        s2_own[s, h, p, g] = total
                    else:
                        s2[s, h, p, g] = total.astype(C2)
                return carry

            lax.fori_loop(0, 8, sum_step, 0)
        c2[s] = go_sent(remote(s2.at[s], r2.at[s], p_yh))

    def c3_issue(s):
        c2[s][0].wait_recv()
        c3[s] = []
        for h in range(2):
            for p in range(2):
                total = s2_own[s, h, p] + r2[s, h, p].astype(F32)
                s3_own[s, h, p] = total
                s3[s, h, p] = total.astype(C3)
            for d in range(3):
                if h == 0:
                    c3[s] += go_sent(remote(s3.at[s, 0, :, xs[d]], r3.at[s, 0, d], p_x[d]))
                else:
                    c3[s] += go_sent(remote(s3.at[s, 1, :, zs[d]], r3.at[s, 1, d], p_z[d]))

    def d1_issue(s):
        for copy in c3[s]:
            copy.wait_recv()
        d1[s] = []
        for h in range(2):
            for p in range(2):
                total = s3_own[s, h, p, x if h == 0 else z]
                for d in range(3):
                    total = total + r3[s, h, d, p].astype(F32)
                if p == 0:
                    wide = pl.ds(pl.multiple_of(first_col(s, yh, h), W), W)
                    total = total - tgt[s // 2, :, wide].astype(F32)
                rp[s, h, p, yh, x, z] = total.astype(BF16)
            ref = rp.at[s, h, :, yh, x, z]
            for d in range(3):
                d1[s] += go_sent(remote(ref, ref, (p_x, p_z)[h][d]))

    def d2_issue(s):
        for copy in d1[s]:
            copy.wait_recv()
        ref0, ref1 = rp.at[s, 0, :, yh, :, z], rp.at[s, 1, :, yh, x]
        d2[s] = go_sent(remote(ref0, ref0, p_yh), remote(ref1, ref1, p_yh))

    def d3_issue(s):
        for copy in d2[s]:
            copy.wait_recv()
        d3[s] = []
        for d in range(2):
            ref0, ref1 = rp.at[s, 0, :, :, :, z], rp.at[s, 1, :, :, x]
            d3[s] += go_sent(remote(ref0, ref0, p_z[d]), remote(ref1, ref1, p_x[d]))

    def d4_issue(s):
        d4[s] = []
        for d in range(2):
            d3[s][2 * d].wait_recv()
            ref = rp.at[s, 0, d, :, :, zs[1 - d]]
            d4[s] += go_sent(remote(ref, ref, p_z[d]))
            d3[s][2 * d + 1].wait_recv()
            ref = rp.at[s, 1, d, :, xs[1 - d]]
            d4[s] += go_sent(remote(ref, ref, p_x[d]))

    partials(0)
    b_core(0)
    b_y(0)
    partials(1)
    b_core(1)
    b_hidden(0)
    b_y(1)
    b_forward(0)
    b_done(0)
    c1_issue(0)
    c1_issue(1)
    b_hidden(1)
    b_forward(1)
    ab1 = []
    for t in range(2):
        ref = ab.at[t, :, q]
        ab1 += go_sent(remote(ref, ref, p_yl), remote(ref, ref, p_core))
    b_done(1)
    goal[0].wait_recv()

    def x_rows(h, half):
        return xg[h, half].reshape(256, 1024)

    def tm_step(i, carry):
        k = i // 4
        half = (i // 2) % 2
        cols = pl.ds(pl.multiple_of((i % 2) * 256, 256), 256)
        tmat[k, pl.ds(pl.multiple_of(half * 256, 256), 256), cols] = (
            dot(x_rows(0, half), st[k, 0:1024, cols]) + dot(x_rows(1, half), st[k, 1024:2048, cols])
        )
        return carry

    def gx_step(i, carry):
        r, t = i // 2, i % 2
        value = dot_nt(x_rows(0, r), x_rows(0, t)) + dot_nt(x_rows(1, r), x_rows(1, t))
        rows = pl.ds(pl.multiple_of(r * 256, 256), 256)
        cols = pl.ds(pl.multiple_of(t * 256, 256), 256)
        high = value.astype(BF16)
        gx[0, rows, cols] = high
        gx[1, rows, cols] = (value - high.astype(F32)).astype(BF16)
        return carry

    xo = pltpu.make_async_copy(xg, x_out, lsem.at[7])
    xo.start()

    def grad(s):
        t = s // 2
        for p in range(2):
            def step(n, carry, p=p):
                rows = pl.ds(pl.multiple_of(n * 256, 256), 256)
                value = jnp.zeros((256, 256), F32)
                for u in range(2):
                    for h in range(2):
                        col = first_col(s, h, u)
                        value = value + dot_nt(rp[s, u, p, h].reshape(256, W), down_w[rows, col:col + W])
                if s % 2:
                    value = value + gacc[t, p, :, rows]
                gacc[t, p, :, rows] = value
                return carry

            lax.fori_loop(0, 2, step, 0)

    e1, e2, e3, e4 = {}, {}, {}, {}

    def e_core(t):
        for i in range(4):
            rows = slice(i * 64, i * 64 + 64)
            pa[t, i] = gacc[t, 1, rows, :] * ab[t, 0, i] + gacc[t, 0, rows, :] * ab[t, 1, i]
        e1[t] = go_sent(remote(pa.at[t, pl.ds((1 - c) * 2, 2)], rg.at[t], p_core))

    def e_y(t):
        e1[t][0].wait_recv()
        sy[t] = (pa[t, qy] + rg[t, 1 - yl]).astype(E_Y)
        e2[t] = go_sent(remote(sy.at[t], ry.at[t], p_yl))

    def e_adjoint(t):
        e2[t][0].wait_recv()
        adj[t, q] = (pa[t, q] + rg[t, yl] + ry[t].astype(F32)).astype(BF16)
        ref = adj.at[t, q]
        e3[t] = go_sent(remote(ref, ref, p_yl), remote(ref, ref, p_core))

    def e_forward(t):
        e3[t][0].wait_recv()
        e4[t] = go_sent(remote(adj.at[t, qy], adj.at[t, qy], p_core))

    def e_done(t):
        e3[t][1].wait_recv()
        e4[t][0].wait_recv()

    def correlate(t):
        for k in range(STORED):
            total = jnp.zeros((1, 128), F32) if t == 0 else stat_c[k:k + 1, :]
            for i in range(2):
                right = adj[t, 2 * i:2 * i + 2].reshape(128, 512).astype(F32)
                if k == 6:
                    left = part[t, 2, 2 * i:2 * i + 2].reshape(128, 512)
                else:
                    left = tmat[k, t * 256 + i * 128:t * 256 + i * 128 + 128, :]
                total = total + fold(left * right)
            stat_c[k:k + 1, :] = total

    def all_sum(stat, slot_y, slot_x):
        mine = (yh * 2 + yl) * 2 + c
        slot_y[mine] = stat[...]
        ref = slot_y.at[mine]
        first = go_sent(*[remote(ref, ref, who) for who in p_yc])
        yield
        for copy in first:
            copy.wait_recv()
        total = slot_y[0]
        for i in range(1, 8):
            total = total + slot_y[i]
        here = x * 4 + z
        slot_x[here] = total
        ref = slot_x.at[here]
        second = go_sent(*[remote(ref, ref, who) for who in p_xz])
        yield
        for copy in second:
            copy.wait_recv()
        total = slot_x[0]
        for i in range(1, 16):
            total = total + slot_x[i]
        yield jnp.sum(total, axis=1, keepdims=True) * (1.0 / (D * FF))

    def gram_range(first, last, accs):
        def step(i, accs):
            row = pl.multiple_of(i * 16, 16)
            accs = list(accs)
            for col in range(4):
                v = [
                    st[k, pl.ds(row, 16), col * 128:(col + 1) * 128].astype(F32)
                    for k in range(STORED)
                ]
                for n, (j, k) in enumerate(PAIRS):
                    prod = v[j] * v[k]
                    accs[n] = accs[n] + prod[0:8] + prod[8:16]
            return tuple(accs)

        return lax.fori_loop(first, last, step, accs)

    accs = tuple(jnp.zeros((8, 128), F32) for _ in PAIRS)
    stages = (c2_issue, c3_issue, d1_issue, d2_issue, d3_issue, d4_issue)
    for turn in range(1, S + 7):
        for n, stage in enumerate(stages):
            if 0 <= turn - 1 - n < S:
                stage(turn - 1 - n)
        if turn + 1 < S:
            c1_issue(turn + 1)
        if turn == 1:
            for copy in ab1:
                copy.wait_recv()
            ref = ab.at[:, :, qy]
            ab2 = go_sent(remote(ref, ref, p_core))
        if turn <= 4:
            lax.fori_loop(6 * turn - 6, 6 * turn, tm_step, 0)
        if turn == 4:
            lax.fori_loop(0, 4, gx_step, 0)
        if 5 <= turn < 9:
            accs = gram_range(32 * turn - 160, 32 * turn - 128, accs)
        if turn == 8:
            for n in range(N_GRAM):
                stat_g[n:n + 1, :] = jnp.sum(accs[n], axis=0, keepdims=True)
            stat_g[N_GRAM:32, :] = jnp.zeros((32 - N_GRAM, 128), F32)
            gram_sum = all_sum(stat_g, slot_gy, slot_gx)
            next(gram_sum)
        if turn == 9:
            next(gram_sum)
        if turn == 9:
            e_y(0)
        if turn == 10:
            e_adjoint(0)
        s = turn - 7
        if 0 <= s < S:
            for copy in d4[s]:
                copy.wait_recv()
            grad(s)
            if s == 0:
                ab2[0].wait_recv()
            if s % 2:
                e_core(s // 2)
    e_forward(0)
    e_y(1)
    e_done(0)
    correlate(0)
    e_adjoint(1)
    means = next(gram_sum)
    gram = {}
    for n, (j, k) in enumerate(PAIRS):
        gram[j, k] = gram[k, j] = means[n:n + 1, :]
    lower = {}
    inverse = []
    for j in range(STORED):
        pivot = gram[j, j]
        for n in range(j):
            pivot = pivot - lower[j, n] * lower[j, n]
        pivot = jnp.sqrt(pivot)
        inverse.append(1.0 / pivot)
        for i in range(j + 1, STORED):
            entry = gram[i, j]
            for n in range(j):
                entry = entry - lower[i, n] * lower[j, n]
            lower[i, j] = entry * inverse[j]
    e_forward(1)
    e_done(1)
    ao = pltpu.make_async_copy(adj, adj_out, lsem.at[8])
    ao.start()

    correlate(1)
    whole = adj[...].reshape(512, 512)
    total = jnp.zeros((1, 128), F32)
    for i in range(2):
        rows = slice(i * 256, i * 256 + 256)
        mixed = dot(gx[0, rows, :], whole) + dot(gx[1, rows, :], whole)
        total = total + fold(mixed * whole[i * 256:i * 256 + 256].astype(F32))
    stat_c[7:8, :] = total

    corr_sum = all_sum(stat_c, slot_cy, slot_cx)
    next(corr_sum)
    next(corr_sum)
    means = next(corr_sum)
    corr = [means[n:n + 1, :] for n in range(STORED)]
    power = means[7:8, :]
    forward = []
    for j in range(STORED):
        running = corr[j]
        for n in range(j):
            running = running - lower[j, n] * forward[n]
        forward.append(running * inverse[j])
    load = [None] * STORED
    for j in reversed(range(STORED)):
        running = forward[j]
        for n in range(j + 1, STORED):
            running = running - lower[n, j] * load[n]
        load[j] = running * inverse[j]
    rest = power
    for j in range(STORED):
        inner = -2.0 * corr[j]
        for k in range(STORED):
            inner = inner + gram[j, k] * load[k]
        rest = rest + load[j] * inner
    rest = jnp.maximum(rest, 0.0)
    scale = 1.0 / jnp.sqrt(rest + 1e-06)
    share = jnp.sqrt((rest + 1e-06) / (power + 1e-06))
    rows = [-(load[j] * scale) for j in range(STORED)] + [scale, share]
    rows = rows + [jnp.zeros((1, 1), F32)] * (16 - len(rows))
    for n in range(16):
        coef_out[n:n + 1, :] = jnp.broadcast_to(rows[n], (1, 128))

    for copy in sent:
        copy.wait_send()
    xo.wait()
    ao.wait()


def final_kernel(coef, x_ref, adj_ref, st_ref, out_ref, share_ref):
    @pl.when(pl.program_id(0) == 0)
    def _():
        share_ref[0] = coef[8, 0]

    left = x_ref[0].reshape(512, x_ref.shape[-1])
    image = lax.dot_general(
        left, adj_ref[...], (((0,), (0,)), ((), ())), preferred_element_type=F32
    )
    total = image * coef[7, 0]
    for k in range(STORED):
        total = total + coef[k, 0] * st_ref[k].astype(F32)
    out_ref[...] = total


def body(inputs, targets, gate_weight, up_weight, down_weight, stored_vectors):
    any_spec = pl.BlockSpec(memory_space=pl.ANY)
    n_copies = 220
    adj, xg, coef = pl.pallas_call(
        comm_kernel,
        out_shape=(
            jax.ShapeDtypeStruct((2, 4, 64, 512), BF16),
            jax.ShapeDtypeStruct((2, 2, 4, 4, 16, 1024), BF16),
            jax.ShapeDtypeStruct((16, 128), F32),
        ),
        in_specs=[any_spec] * 6,
        out_specs=(any_spec, any_spec, pl.BlockSpec(memory_space=pltpu.VMEM)),
        scratch_shapes=[
            pltpu.VMEM((2, 2, 4, 4, 16, 1024), BF16),
            pltpu.VMEM((2, 16, 2048), BF16),
            pltpu.VMEM((2048, 512), BF16),
            pltpu.VMEM((2048, 512), BF16),
            pltpu.VMEM((512, 2048), BF16),
            pltpu.VMEM((STORED, 2048, 512), BF16),
            pltpu.VMEM((2, 3, 4, 4, 16, 512), F32),
            pltpu.VMEM((2, 3, 2, 4, 16, 512), F32),
            pltpu.VMEM((2, 3, 4, 16, 512), B_Y),
            pltpu.VMEM((2, 3, 4, 16, 512), B_Y),
            pltpu.VMEM((STORED - 1, 512, 512), F32),
            pltpu.VMEM((2, 512, 512), BF16),
            pltpu.VMEM((2, 2, 4, 64, 512), BF16),
            pltpu.VMEM((2, 2, 4, 64, 512), F32),
            pltpu.VMEM((S, 2, 4, 4, 4, 16, W), C1),
            pltpu.VMEM((S, 2, 3, 4, 4, 16, W), C1),
            pltpu.VMEM((S, 2, 2, 4, 16, W), C2),
            pltpu.VMEM((S, 2, 2, 4, 16, W), F32),
            pltpu.VMEM((S, 2, 2, 4, 16, W), C2),
            pltpu.VMEM((S, 2, 2, 4, 16, W), C3),
            pltpu.VMEM((S, 2, 2, 4, 16, W), F32),
            pltpu.VMEM((S, 2, 3, 2, 16, W), C3),
            pltpu.VMEM((S, 2, 2, 2, 4, 4, 16, W), BF16),
            pltpu.VMEM((2, 2, 256, 512), F32),
            pltpu.VMEM((2, 4, 64, 512), F32),
            pltpu.VMEM((2, 2, 64, 512), F32),
            pltpu.VMEM((2, 64, 512), E_Y),
            pltpu.VMEM((2, 64, 512), E_Y),
            pltpu.VMEM((2, 4, 64, 512), BF16),
            pltpu.VMEM((32, 128), F32),
            pltpu.VMEM((8, 32, 128), F32),
            pltpu.VMEM((16, 32, 128), F32),
            pltpu.VMEM((8, 128), F32),
            pltpu.VMEM((8, 8, 128), F32),
            pltpu.VMEM((16, 8, 128), F32),
            pltpu.SemaphoreType.DMA((9,)),
            pltpu.SemaphoreType.DMA((n_copies,)),
            pltpu.SemaphoreType.DMA((n_copies,)),
        ],
        compiler_params=pltpu.CompilerParams(
            collective_id=0, has_side_effects=True, vmem_limit_bytes=62 * 2**20
        ),
        name="exchange",
    )(inputs, targets, gate_weight, up_weight, down_weight, stored_vectors)

    tile = 1024
    per_half = 1024 // tile
    next_vector, share = pl.pallas_call(
        final_kernel,
        grid=(2048 // tile,),
        out_shape=(
            jax.ShapeDtypeStruct((2048, 512), F32),
            jax.ShapeDtypeStruct((1,), F32),
        ),
        in_specs=[
            pl.BlockSpec(memory_space=pltpu.SMEM),
            pl.BlockSpec((1, 512, tile), lambda i: (i // per_half, 0, i % per_half)),
            pl.BlockSpec((512, 512), lambda i: (0, 0)),
            pl.BlockSpec((STORED, tile, 512), lambda i: (0, i, 0)),
        ],
        out_specs=(
            pl.BlockSpec((tile, 512), lambda i: (i, 0)),
            pl.BlockSpec(memory_space=pltpu.SMEM),
        ),
        compiler_params=pltpu.CompilerParams(vmem_limit_bytes=60 * 2**20),
        name="finish",
    )(coef, xg.reshape(2, 512, 1024), adj.reshape(512, 512), stored_vectors)
    return next_vector, share


def solution(mesh):
    return jax.shard_map(
        body,
        mesh=mesh,
        in_specs=(
            P("ffn", "mp"),
            P("ffn", "mp"),
            P("mp", "ffn"),
            P("mp", "ffn"),
            P("ffn", "mp"),
            P(None, "mp", "ffn"),
        ),
        out_specs=(P("mp", "ffn"), P()),
        check_vma=False,
    )
```
